512 devices in a mesh: load: 32 (over x, y), tm: 16 (over z, core).
Axes of the slice: x: 4, y: 8, z: 8, core: 2. Of those that a mesh axis runs over, the one named last changes fastest.
Arguments:
- frames: bfloat16 [16, 1024, 8, 24, 256], P('tm', 'load'), may hold values from -6 to 6
- counts: int32 [16, 1024], P('tm', 'load'), may hold values from 3 to 8
- dest: int32 [1024], P('load'), may hold values from 0 to 1023, as said below
- first_weight: bfloat16 [3, 256, 256], replicated, may hold values from -0.21875 to 0.21875
- second_weight: bfloat16 [3, 256, 256], replicated, may hold values from -0.21875 to 0.21875
- gain: float32 [256], replicated, may hold values from 0.5 to 2
- bias: float32 [256], replicated, may hold values from -3 to 3
Outputs:
- latents: bfloat16 [16, 1024, 2, 24, 256], P('tm', 'load')
The draws below stay inside these ranges and needn't reach their ends.
Inputs may be any that keep to these rules, and one draw needn't show every extreme that they name: dest is a permutation; video c goes to owner dest // 32, the load index that holds output rows of that block. A loader sends each owner none or exactly 2 of its videos, and an owner's slots 2 i and 2 i + 1 hold videos of one loader.
All inputs are finite; a program needn't handle non-finite values.
Results may differ from the reference program's by a relative error of at most 0.009.
Values may be sent and summed in bfloat16 or wider, within the bound.
A program may use at most 64 MiB of HBM per device.

```python
import math
import jax
import jax.numpy as jnp
from jax import lax

C = 256
FMAX = 8
P_SIZE = 24
CH_DEV = 32
NC = 1024
VCHUNKS = 16


def draw_dest(key, part):
    key = jax.random.fold_in(key, 7)
    first_key, second_key, third_key = jax.random.split(key, 3)
    loaders = NC // CH_DEV
    sigma = jax.random.permutation(first_key, loaders)
    tau = jax.random.permutation(second_key, loaders)
    scores = jax.random.randint(third_key, (loaders, CH_DEV), 0, 1048576) * CH_DEV + jnp.arange(CH_DEV, dtype=jnp.int32)[None, :]
    ranks = jnp.argsort(jnp.argsort(scores, axis=1), axis=1).reshape(-1)
    loader = jnp.arange(NC, dtype=jnp.int32) // CH_DEV
    pair = ranks // 2
    owner = tau[(sigma[loader] + pair) % loaders]
    return (owner * CH_DEV + 2 * pair + ranks % 2).astype(jnp.int32)


def set_ends(array, stream_key, smallest, high):
    spot = [jax.random.randint(jax.random.fold_in(stream_key, axis), (), 0, length) for axis, length in enumerate(array.shape)]
    main_axis = array.shape.index(max(array.shape))
    beside = spot[:main_axis] + [(spot[main_axis] + 1) % array.shape[main_axis]] + spot[main_axis + 1:]
    return array.at[tuple(spot)].set(smallest).at[tuple(beside)].set(high)


def shard_levels(stream_key, shape, shards, smallest, largest):
    factor_of = 1.0
    for axis_at, parts in shards:
        steps = jax.random.uniform(jax.random.fold_in(jax.random.fold_in(stream_key, 6), axis_at), (parts,), jnp.float32, smallest / len(shards), largest / len(shards))
        factor_of = factor_of * jnp.repeat(jnp.exp(steps), shape[axis_at] // parts).reshape((-1,) + (1,) * (len(shape) - 1 - axis_at))
    return factor_of


def scatter_about(key, shape, width, bound, shards=(), held_as=jnp.bfloat16):
    result = width * jax.random.normal(key, shape, jnp.float32)
    if shards:
        result = result * shard_levels(key, shape, shards, -0.22, 0.18)
    return jnp.clip(result, -bound, bound).astype(held_as)


def setup_inputs(seed: int = 0) -> dict:
    streams_of = jax.random.split(jax.random.key(seed), 8)
    frames = scatter_about(streams_of[0], (VCHUNKS, NC, FMAX, P_SIZE, C), 1.0, 6.0, ((0, 16), (1, 32)))
    counts = set_ends(jax.random.randint(streams_of[1], (VCHUNKS, NC), 3, FMAX + 1), jax.random.fold_in(streams_of[1], 1), 3, FMAX).astype(jnp.int32)
    dest = draw_dest(jax.random.fold_in(streams_of[7], 71), 0)
    first_weight = scatter_about(streams_of[3], (3, C, C), (3 * C) ** -0.5, 0.21875)
    second_weight = scatter_about(streams_of[4], (3, C, C), (3 * C) ** -0.5, 0.21875)
    gain = jnp.clip(jnp.exp(jax.random.uniform(streams_of[5], (C,), jnp.float32, math.log(0.5), math.log(2.0))), 0.5, 2.0)
    bias = scatter_about(streams_of[6], (C,), 0.5, 3.0, (), jnp.float32)
    return {"frames": frames, "counts": counts, "dest": dest, "first_weight": first_weight, "second_weight": second_weight, "gain": gain, "bias": bias}


def last_two(block, count):
    index = (count[:, None] - 2 + jnp.arange(2, dtype=jnp.int32)[None, :]).astype(jnp.int32)
    return jnp.take_along_axis(block, index[:, :, None, None], axis=1)

def causal_layer(block, context, weight):
    extended = jnp.concatenate([context, block], axis=1).astype(jnp.float32)
    outlen = block.shape[1] // 2
    total = jnp.zeros((block.shape[0], outlen, block.shape[2], weight.shape[2]), jnp.float32)
    for tap in range(3):
        taken = extended[:, tap:tap + 2 * outlen - 1:2]
        total = total + jnp.einsum('kjpc,cd->kjpd', taken, weight[tap].astype(jnp.float32))
    return total

def live_mask(count, length, step):
    return (step * jnp.arange(length, dtype=jnp.int32)[None, :] < count[:, None])[:, :, None, None]

def reference(frames, counts, dest, first_weight, second_weight, gain, bias):
    groups = NC // CH_DEV

    def step(carry, inputs):
        raw_ctx, prev1, prev2, prevn, norm_ctx = carry
        block, count = inputs
        block = jnp.where(live_mask(count, FMAX, 1), block, jnp.zeros_like(block))
        first = jax.nn.silu(causal_layer(block, raw_ctx, first_weight))
        first = jnp.where(live_mask(count, FMAX // 2, 2), first, 0.0).astype(jnp.bfloat16)
        half = (count + 1) // 2
        values = first.astype(jnp.float32)
        sum1 = prev1 + lax.optimization_barrier(jnp.sum(values, axis=(1, 2)))
        sum2 = prev2 + lax.optimization_barrier(jnp.sum(values * values, axis=(1, 2)))
        num = prevn + (half * P_SIZE).astype(jnp.float32)
        mean = sum1 / num[:, None]
        var = sum2 / num[:, None] - mean * mean
        normed = (values - mean[:, None, None, :]) * lax.rsqrt(var + 1e-05)[:, None, None, :] * gain
        normed = jnp.where(live_mask(count, FMAX // 2, 2), normed, 0.0).astype(jnp.bfloat16)
        second = causal_layer(normed, norm_ctx, second_weight) + bias
        encoded = jnp.where(live_mask(half, FMAX // 4, 2), second, 0.0).astype(jnp.bfloat16)
        return ((last_two(block, count), sum1, sum2, num, last_two(normed, half)), encoded)

    def one_group(index):
        start = (index * CH_DEV).astype(jnp.int32)
        block = lax.dynamic_slice_in_dim(frames, start, CH_DEV, 1)
        count = lax.dynamic_slice_in_dim(counts, start, CH_DEV, 1)
        context = jnp.zeros((CH_DEV, 2, P_SIZE, C), jnp.bfloat16)
        stats = jnp.zeros((CH_DEV, C), jnp.float32)
        init = (context, stats, stats, jnp.zeros((CH_DEV,), jnp.float32), context)
        _, encoded = lax.scan(step, init, (block, count))
        return encoded
    encoded = lax.map(one_group, jnp.arange(groups, dtype=jnp.int32))
    encoded = jnp.transpose(encoded, (1, 0, 2, 3, 4, 5)).reshape(VCHUNKS, NC, FMAX // 4, P_SIZE, C)
    return jnp.zeros_like(encoded).at[:, dest].set(encoded)
```

```python
import functools

import jax
import jax.numpy as jnp
from jax import lax
from jax.experimental import pallas as pl
from jax.experimental.pallas import tpu as pltpu
from jax.sharding import PartitionSpec as P

F32 = jnp.float32
BF16 = jnp.bfloat16
MESH = pl.DeviceIdType.MESH


def flat(x):
    videos, places, channels = x.shape
    return x.astype(F32).reshape(videos * places, channels).astype(BF16)


def dot(a, b):
    return jnp.dot(a, b, preferred_element_type=F32)


def silu(x):
    h = 0.5 * x
    return h + h * jnp.tanh(h)


def kernel(
    loads,
    spans,
    group,
    cnt_s,
    pack_s,
    cnt_v,
    dest_v,
    frames,
    w1,
    w2,
    gain,
    bias,
    out,
    tail,
    t1_send,
    t1_recv,
    t2_send,
    t2_recv,
    first,
    acc1,
    acc2,
    a_send,
    a_recv,
    b_send,
    b_recv,
    c_send,
    c_recv,
    mean_v,
    scale_v,
    enc_0,
    enc_1,
    stage,
    recv_0,
    recv_1,
    d_send,
    d_recv,
    table,
    sem_t,
    sem_b_send,
    sem_b_recv,
    sem_d_send,
    sem_d_recv,
    sem_x_send,
    sem_x_recv,
):
    videos, places, channels = frames.shape[0], frames.shape[2], frames.shape[3]
    length = frames.shape[1]
    chips = spans // 2
    half_c = channels // 2
    rows = group * places
    pairs = videos // 2
    me = lax.axis_index("load")
    t = lax.axis_index("tm")
    z = t // 2
    core = t % 2
    other = z * 2 + 1 - core
    after = lax.rem(t + 1, spans)
    beyond = lax.rem(t + jnp.where(core == 0, spans - 1, 1), spans)

    barrier = pltpu.get_barrier_semaphore()

    def greet(load, place):
        pl.semaphore_signal(barrier, inc=1, device_id=(load, place), device_id_type=MESH)

    greet(me, other)
    greet(me, beyond)

    @pl.loop(1, chips)
    def _(s):
        greet(me, lax.rem(z + s, chips) * 2 + core)

    @pl.loop(1, loads)
    def _(s):
        greet(lax.rem(me + s, loads), t)

    @pl.loop(0, videos)
    def _(v):
        tail[0, v] = frames[v, jnp.clip(cnt_s[0, v] - 2, 0, length - 1)]
        tail[1, v] = frames[v, jnp.clip(cnt_s[0, v] - 1, 0, length - 1)]

    @pl.loop(0, videos // group)
    def _(g):
        at = pl.ds(g * group, group)
        lhs = jnp.concatenate([flat(tail[0, at]), flat(tail[1, at])], axis=1)
        t1_send[pl.ds(pl.multiple_of(g * rows, rows), rows)] = dot(lhs, w1[: 2 * channels]).astype(BF16)

    lanes = 128
    row = jnp.pad(dest_v[...], ((0, 7), (0, lanes - videos)), constant_values=-1)
    d_send[...] = row

    pl.semaphore_wait(barrier, 1 + 1 + (chips - 1) + (loads - 1))

    def remote(src, dst, ss, rs, load, place):
        return pltpu.make_async_remote_copy(
            src_ref=src, dst_ref=dst, send_sem=ss, recv_sem=rs, device_id=(load, place), device_id_type=MESH
        )

    t1 = remote(t1_send, t1_recv, sem_t.at[0], sem_t.at[1], me, after)
    t1.start()

    @pl.loop(1, loads)
    def _(s):
        remote(d_send, d_recv.at[me], sem_d_send.at[s], sem_d_recv.at[s], lax.rem(me + s, loads), t).start()

    d_recv[me] = row

    def column(values):
        r = lax.broadcasted_iota(jnp.int32, (videos, videos), 0)
        c = lax.broadcasted_iota(jnp.int32, (videos, videos), 1)
        return jnp.sum(jnp.where(r == c, values, 0), axis=1, keepdims=True)

    counts_row = cnt_v[...]

    def add_sums(g, at, values, fresh):
        tiles = values.reshape(group, places // 8, 8, channels)
        s1 = jnp.sum(tiles, axis=1)
        s2 = jnp.sum(tiles * tiles, axis=1)
        if fresh:
            acc1[at] = s1
            acc2[at] = s2
        else:
            acc1[at] += s1
            acc2[at] += s2

    def group_live(g, step, limit_of):
        parts = [limit_of(cnt_s[0, g * group + i]) > step for i in range(group)]
        return parts

    def masked(value, flags):
        pieces = value.reshape(group, places, channels)
        return jnp.concatenate(
            [jnp.where(flags[i], pieces[i : i + 1], 0.0) for i in range(group)], axis=0
        )

    @pl.loop(0, videos // group)
    def _(g):
        at = pl.ds(g * group, group)
        place = pl.ds(pl.multiple_of(g * rows, rows), rows)
        for j in range(1, 4):
            lhs = jnp.concatenate([flat(frames[at, 2 * j - 2 + k]) for k in range(3)], axis=1)
            value = masked(silu(dot(lhs, w1[...])), group_live(g, 2 * j, lambda n: n))
            value = value.reshape(rows, channels).astype(BF16)
            first[j, place] = value
            add_sums(g, at, value.astype(F32), j == 1)

    t1.wait_recv()

    @pl.loop(0, videos // group)
    def _(g):
        at = pl.ds(g * group, group)
        place = pl.ds(pl.multiple_of(g * rows, rows), rows)
        part = jnp.where(t > 0, t1_recv[place].astype(F32), 0.0)
        value = silu(part + dot(flat(frames[at, 0]), w1[2 * channels :])).astype(BF16)
        first[0, place] = value
        add_sums(g, at, value.astype(F32), False)

    s1 = jnp.sum(acc1[...], axis=1)
    s2 = jnp.sum(acc2[...], axis=1)
    num = (((counts_row + 1) // 2) * places).astype(F32)
    num = jnp.pad(num, ((0, 7), (0, lanes - videos)))
    low = core == 0
    enc = (enc_0, enc_1)
    recv = (recv_0, recv_1)

    def mine(x):
        return jnp.where(low, x[:, :half_c], x[:, half_c:])

    def others(x):
        return jnp.where(low, x[:, half_c:], x[:, :half_c])

    a_send[...] = jnp.concatenate([others(s1), others(s2), num], axis=0)
    a_copy = remote(a_send, a_recv, sem_t.at[2], sem_t.at[3], me, other)
    a_copy.start()
    own = jnp.concatenate([mine(s1), mine(s2), num], axis=0)
    a_copy.wait_recv()
    theirs = a_recv[...]
    chip = own + theirs
    b_send[...] = chip

    @pl.loop(1, chips)
    def _(s):
        remote(
            b_send, b_recv.at[s - 1], sem_b_send.at[s - 1], sem_b_recv.at[s - 1], me, lax.rem(z + s, chips) * 2 + core
        ).start()

    even = jnp.where(low, own, theirs)
    base = jnp.zeros_like(own)
    for s in range(1, chips):
        remote(b_send, b_recv.at[s - 1], sem_b_send.at[s - 1], sem_b_recv.at[s - 1], me, other).wait_recv()
        base = base + jnp.where(z >= s, b_recv[s - 1], 0.0)

    my_gain = mine(gain[...])

    def finish(total):
        count = column(total[2 * videos : 2 * videos + 1, :videos])
        mean = total[:videos] / count
        var = total[videos : 2 * videos] / count - mean * mean
        return jnp.concatenate([mean, lax.rsqrt(var + 1e-05) * my_gain], axis=0)

    on_even = finish(base + even)
    on_odd = finish(base + chip)
    c_send[...] = jnp.where(low, on_odd, on_even)
    c_copy = remote(c_send, c_recv, sem_t.at[4], sem_t.at[5], me, other)
    c_copy.start()
    here = jnp.where(low, on_even, on_odd)
    c_copy.wait_recv()
    there = c_recv[...]
    both = jnp.concatenate([jnp.where(low, here, there), jnp.where(low, there, here)], axis=1)
    mean_v[...] = both[:videos]
    scale_v[...] = both[videos:]

    @pl.loop(0, videos // group)
    def _(g):
        at = pl.ds(pl.multiple_of(g * group, group), group)
        place = pl.ds(pl.multiple_of(g * rows, rows), rows)
        mean = mean_v[at][:, None, :]
        scale = scale_v[at][:, None, :]
        normed = []
        for j in range(4):
            value = first[j, place].astype(F32).reshape(group, places, channels)
            value = (value - mean) * scale
            normed.append(value)
            first[j, place] = value.reshape(rows, channels).astype(BF16)
        ends = []
        for k in range(2):
            pieces = []
            for i in range(group):
                n = (cnt_s[0, g * group + i] + 1) // 2
                pieces.append(
                    jnp.where(
                        n == 2,
                        normed[k][i : i + 1],
                        jnp.where(n == 3, normed[k + 1][i : i + 1], normed[k + 2][i : i + 1]),
                    )
                )
            ends.append(jnp.concatenate(pieces, axis=0).reshape(rows, channels).astype(BF16))
        t2_send[place] = dot(jnp.concatenate(ends, axis=1), w2[: 2 * channels]).astype(BF16)

    t2 = remote(t2_send, t2_recv, sem_t.at[6], sem_t.at[7], me, after)
    t2.start()

    def exchange(i):
        stage[i, me, 0] = enc[i][pack_s[2 * me]]
        stage[i, me, 1] = enc[i][pack_s[2 * me + 1]]
        recv[i][me] = stage[i, me]

        @pl.loop(1, loads)
        def _(s):
            to = lax.rem(me + s, loads)
            stage[i, to, 0] = enc[i][pack_s[2 * to]]
            stage[i, to, 1] = enc[i][pack_s[2 * to + 1]]
            remote(stage.at[i, to], recv[i].at[me], sem_x_send.at[i, s], sem_x_recv.at[i, s], to, t).start()

    @pl.loop(0, videos // group)
    def _(g):
        at = pl.ds(g * group, group)
        place = pl.ds(pl.multiple_of(g * rows, rows), rows)
        lhs = jnp.concatenate([first[j, place] for j in range(3)], axis=1)
        value = masked(dot(lhs, w2[...]) + bias[...], group_live(g, 2, lambda n: (n + 1) // 2))
        enc_1[at] = value.astype(BF16)

    exchange(1)
    t2.wait_recv()

    @pl.loop(0, videos // group)
    def _(g):
        at = pl.ds(g * group, group)
        place = pl.ds(pl.multiple_of(g * rows, rows), rows)
        part = jnp.where(t > 0, t2_recv[place].astype(F32), 0.0)
        value = part + dot(first[0, place], w2[2 * channels :]) + bias[...]
        enc_0[at] = value.reshape(group, places, channels).astype(BF16)

    exchange(0)

    @pl.loop(1, loads)
    def _(s):
        remote(
            d_send, d_recv.at[lax.rem(me + loads - s, loads)], sem_d_send.at[s], sem_d_recv.at[s], me, other
        ).wait_recv()

    known = d_recv[...][:, 0, :]
    loader = lax.broadcasted_iota(jnp.int32, known.shape, 0)
    for i in range(pairs):
        table[i] = jnp.clip(jnp.sum(jnp.where(known == me * videos + 2 * i, loader, 0)), 0, loads - 1)

    for i in (1, 0):

        @pl.loop(1, loads)
        def _(s):
            remote(
                stage.at[i, 0],
                recv[i].at[lax.rem(me + loads - s, loads)],
                sem_x_send.at[i, s],
                sem_x_recv.at[i, s],
                me,
                other,
            ).wait_recv()

        @pl.loop(0, pairs)
        def _(q):
            out[2 * q, i] = recv[i][table[q], 0]
            out[2 * q + 1, i] = recv[i][table[q], 1]

    t1.wait_send()
    t2.wait_send()
    a_copy.wait_send()
    c_copy.wait_send()

    @pl.loop(1, chips)
    def _(s):
        remote(b_send, b_recv.at[s - 1], sem_b_send.at[s - 1], sem_b_recv.at[s - 1], me, other).wait_send()

    @pl.loop(1, loads)
    def _(s):
        remote(d_send, d_recv.at[me], sem_d_send.at[s], sem_d_recv.at[s], me, other).wait_send()
        for i in range(2):
            remote(stage.at[i, 0], recv[i].at[me], sem_x_send.at[i, s], sem_x_recv.at[i, s], me, other).wait_send()


def body(loads, spans, frames, counts, dest, first_weight, second_weight, gain, bias):
    videos, length, places, channels = frames.shape[1:]
    group = min(8, videos)
    rows = videos * places
    chips = spans // 2
    slot = dest // videos * 2 + dest % 2
    hit = slot[None, :] == jnp.arange(2 * loads, dtype=jnp.int32)[:, None]
    pack = jnp.sum(jnp.where(hit, jnp.arange(videos, dtype=jnp.int32)[None, :], 0), axis=1)
    vmem = pl.BlockSpec(memory_space=pltpu.VMEM)
    smem = pl.BlockSpec(memory_space=pltpu.SMEM)
    message = (2 * videos + 8, 128)
    result = pl.pallas_call(
        functools.partial(kernel, loads, spans, group),
        out_shape=jax.ShapeDtypeStruct((videos, 2, places, channels), BF16),
        in_specs=[smem, smem] + [vmem] * 7,
        out_specs=vmem,
        scratch_shapes=[
            pltpu.VMEM((2, videos, places, channels), BF16),
            pltpu.VMEM((rows, channels), BF16),
            pltpu.VMEM((rows, channels), BF16),
            pltpu.VMEM((rows, channels), BF16),
            pltpu.VMEM((rows, channels), BF16),
            pltpu.VMEM((4, rows, channels), BF16),
            pltpu.VMEM((videos, 8, channels), F32),
            pltpu.VMEM((videos, 8, channels), F32),
            pltpu.VMEM(message, F32),
            pltpu.VMEM(message, F32),
            pltpu.VMEM(message, F32),
            pltpu.VMEM((chips - 1,) + message, F32),
            pltpu.VMEM((2 * videos, 128), F32),
            pltpu.VMEM((2 * videos, 128), F32),
            pltpu.VMEM((videos, channels), F32),
            pltpu.VMEM((videos, channels), F32),
            pltpu.VMEM((videos, places, channels), BF16),
            pltpu.VMEM((videos, places, channels), BF16),
            pltpu.VMEM((2, loads, 2, places, channels), BF16),
            pltpu.VMEM((loads, 2, places, channels), BF16),
            pltpu.VMEM((loads, 2, places, channels), BF16),
            pltpu.VMEM((8, 128), jnp.int32),
            pltpu.VMEM((loads, 8, 128), jnp.int32),
            pltpu.SMEM((videos // 2,), jnp.int32),
            pltpu.SemaphoreType.DMA((8,)),
            pltpu.SemaphoreType.DMA((chips - 1,)),
            pltpu.SemaphoreType.DMA((chips - 1,)),
            pltpu.SemaphoreType.DMA((loads,)),
            pltpu.SemaphoreType.DMA((loads,)),
            pltpu.SemaphoreType.DMA((2, loads)),
            pltpu.SemaphoreType.DMA((2, loads)),
        ],
        compiler_params=pltpu.CompilerParams(
            collective_id=0, has_side_effects=True, vmem_limit_bytes=48 * 1024 * 1024
        ),
    )(
        counts,
        pack,
        counts,
        dest.reshape(1, videos),
        frames[0],
        first_weight.reshape(3 * channels, channels),
        second_weight.reshape(3 * channels, channels),
        gain.reshape(1, channels),
        bias.reshape(1, channels),
    )
    return result[None]


def solution(mesh):
    loads, spans = mesh.shape["load"], mesh.shape["tm"]
    return jax.shard_map(
        functools.partial(body, loads, spans),
        mesh=mesh,
        in_specs=(
            P("tm", "load", None, None, None),
            P("tm", "load"),
            P("load"),
            P(),
            P(),
            P(),
            P(),
        ),
        out_specs=P("tm", "load", None, None, None),
        check_vma=False,
    )
```

```python
import functools

import jax
import jax.numpy as jnp
from jax import lax
from jax.experimental import pallas as pl
from jax.experimental.pallas import tpu as pltpu
from jax.sharding import PartitionSpec as P

F32 = jnp.float32
BF16 = jnp.bfloat16
MESH = pl.DeviceIdType.MESH


def flat(x):
    videos, places, channels = x.shape
    return x.astype(F32).reshape(videos * places, channels).astype(BF16)


def dot(a, b):
    return jnp.dot(a, b, preferred_element_type=F32)


def silu(x):
    h = 0.5 * x
    return h + h * jnp.tanh(h)


def kernel(
    loads,
    spans,
    group,
    counts_hbm,
    dest_hbm,
    frames_hbm,
    w1_hbm,
    w2_hbm,
    gain_hbm,
    bias_hbm,
    out,
    cnt_s,
    cnt_v,
    dest_v,
    frames,
    w1,
    w2,
    gain,
    bias,
    pack_v,
    pack_s,
    tail,
    t1_send,
    t1_recv,
    t2_send,
    t2_recv,
    first,
    acc1,
    acc2,
    a_send,
    a_recv,
    b_send,
    b_recv,
    c_send,
    c_recv,
    mean_v,
    scale_v,
    enc_0,
    enc_1,
    stage,
    recv_0,
    recv_1,
    d_send,
    d_recv,
    table,
    sem_in,
    sem_t,
    sem_c_send,
    sem_c_recv,
    sem_a_send,
    sem_a_recv,
    sem_b_send,
    sem_b_recv,
    sem_s_send,
    sem_s_recv,
    sem_x_send,
    sem_x_recv,
):
    videos, places, channels = frames.shape[0], frames.shape[2], frames.shape[3]
    length = frames.shape[1]
    teams = spans // 4
    quarter = channels // 4
    rows = group * places
    pairs = videos // 2
    me = lax.axis_index("load")
    t = lax.axis_index("tm")
    team = t // 4
    seat = t % 4
    after = lax.rem(t + 1, spans)
    beyond = lax.rem(t + jnp.where(seat == 0, spans - 1, 1), spans)
    edge = jnp.logical_or(seat == 0, seat == 3)

    pieces = 4
    part = videos // pieces
    fetches = [
        pltpu.make_async_copy(a, b, sem_in.at[i])
        for i, (a, b) in enumerate(
            [(counts_hbm, cnt_s), (counts_hbm, cnt_v), (dest_hbm, dest_v)]
            + [(frames_hbm.at[pl.ds(q * part, part)], frames.at[pl.ds(q * part, part)]) for q in range(pieces)]
            + [(w1_hbm, w1), (w2_hbm, w2), (gain_hbm, gain), (bias_hbm, bias)]
        )
    ]
    for fetch in fetches:
        fetch.start()

    enc = (enc_0, enc_1)
    recv = (recv_0, recv_1)
    barrier = pltpu.get_barrier_semaphore()

    def greet(load, place):
        pl.semaphore_signal(barrier, inc=1, device_id=(load, place), device_id_type=MESH)

    @pl.when(edge)
    def _():
        greet(me, beyond)

    for s in range(1, 4):
        greet(me, team * 4 + lax.rem(seat + s, 4))
    for s in range(1, teams):
        greet(me, lax.rem(team + s, teams) * 4 + seat)

    @pl.loop(1, loads)
    def _(s):
        greet(lax.rem(me + s, loads), t)

    for fetch in fetches[:-3]:
        fetch.wait()

    @pl.loop(0, videos)
    def _(v):
        tail[0, v] = frames[v, jnp.clip(cnt_s[0, v] - 2, 0, length - 1)]
        tail[1, v] = frames[v, jnp.clip(cnt_s[0, v] - 1, 0, length - 1)]

    @pl.loop(0, videos // group)
    def _(g):
        at = pl.ds(g * group, group)
        lhs = jnp.concatenate([flat(tail[0, at]), flat(tail[1, at])], axis=1)
        t1_send[pl.ds(pl.multiple_of(g * rows, rows), rows)] = dot(lhs, w1[: 2 * channels]).astype(BF16)

    lanes = 128
    row = jnp.pad(dest_v[...], ((0, 7), (0, lanes - videos)), constant_values=-1)
    d_send[...] = row

    pl.semaphore_wait(barrier, 3 + (teams - 1) + (loads - 1) + jnp.where(edge, 1, 0))

    def remote(src, dst, ss, rs, load, place):
        return pltpu.make_async_remote_copy(
            src_ref=src, dst_ref=dst, send_sem=ss, recv_sem=rs, device_id=(load, place), device_id_type=MESH
        )

    def context(g):
        place = pl.ds(pl.multiple_of(g * rows, rows), rows)
        return remote(t1_send.at[place], t1_recv.at[place], sem_c_send.at[g], sem_c_recv.at[g], me, after)

    for g in range(videos // group):
        context(g).start()

    d_recv[me] = row

    def column(values):
        r = lax.broadcasted_iota(jnp.int32, (videos, videos), 0)
        c = lax.broadcasted_iota(jnp.int32, (videos, videos), 1)
        return jnp.sum(jnp.where(r == c, values, 0), axis=1, keepdims=True)

    for fetch in fetches[-3:]:
        fetch.wait()
    counts_row = cnt_v[...]

    place_of = column(dest_v[...])
    place_of = place_of // videos * 2 + place_of % 2
    lane = lax.broadcasted_iota(jnp.int32, (videos, 128), 1)
    video = lax.broadcasted_iota(jnp.int32, (videos, 128), 0)
    pack_v[...] = jnp.clip(jnp.sum(jnp.where(place_of == lane, video, 0), axis=0, keepdims=True), 0, videos - 1)
    to_scalars = pltpu.make_async_copy(pack_v, pack_s, sem_in.at[len(fetches)])
    to_scalars.start()

    def add_sums(g, at, values, fresh):
        tiles = values.reshape(group, places // 8, 8, channels)
        s1 = jnp.sum(tiles, axis=1)
        s2 = jnp.sum(tiles * tiles, axis=1)
        if fresh:
            acc1[at] = s1
            acc2[at] = s2
        else:
            acc1[at] += s1
            acc2[at] += s2

    def group_live(g, step, limit_of):
        parts = [limit_of(cnt_s[0, g * group + i]) > step for i in range(group)]
        return parts

    def masked(value, flags):
        pieces = value.reshape(group, places, channels)
        return jnp.concatenate(
            [jnp.where(flags[i], pieces[i : i + 1], 0.0) for i in range(group)], axis=0
        )

    @pl.loop(0, videos // group)
    def _(g):
        at = pl.ds(g * group, group)
        place = pl.ds(pl.multiple_of(g * rows, rows), rows)
        for j in range(1, 4):
            lhs = jnp.concatenate([flat(frames[at, 2 * j - 2 + k]) for k in range(3)], axis=1)
            value = masked(silu(dot(lhs, w1[...])), group_live(g, 2 * j, lambda n: n))
            value = value.reshape(rows, channels).astype(BF16)
            first[j, place] = value
            add_sums(g, at, value.astype(F32), j == 1)

    @pl.loop(1, loads)
    def _(s):
        remote(d_send, d_recv.at[me], sem_t.at[2], sem_t.at[3], lax.rem(me + s, loads), t).start()

    to_scalars.wait()

    @pl.loop(0, videos // group)
    def _(g):
        at = pl.ds(g * group, group)
        place = pl.ds(pl.multiple_of(g * rows, rows), rows)
        context(g).wait_recv()
        part = jnp.where(t > 0, t1_recv[place].astype(F32), 0.0)
        value = silu(part + dot(flat(frames[at, 0]), w1[2 * channels :])).astype(BF16)
        first[0, place] = value
        add_sums(g, at, value.astype(F32), False)

    s1 = jnp.sum(acc1[...], axis=1)
    s2 = jnp.sum(acc2[...], axis=1)
    num = (((counts_row + 1) // 2) * places).astype(F32)
    num = jnp.pad(num, ((0, 7), (0, lanes - videos)))

    def parts(x):
        return [x[:, r * quarter : (r + 1) * quarter] for r in range(4)]

    for r, (p1, p2) in enumerate(zip(parts(s1), parts(s2))):
        a_send[r] = jnp.concatenate([jnp.concatenate([p1, p2], axis=1), num], axis=0)

    def mates(source, target, ss, rs):
        made = []
        for s in range(1, 4):
            mate = lax.rem(seat + s, 4)
            made.append(
                remote(source.at[mate], target.at[seat], ss.at[s - 1], rs.at[s - 1], me, team * 4 + mate)
            )
        return made

    a_copies = mates(a_send, a_recv, sem_a_send, sem_a_recv)
    for copy in a_copies:
        copy.start()
    a_recv[seat] = a_send[seat]
    my_gain = sum(jnp.where(seat == r, g, 0.0) for r, g in enumerate(parts(gain[...])))
    my_gain = jnp.concatenate([my_gain, my_gain], axis=1)
    for s in range(1, 4):
        from_mate = lax.rem(seat + 4 - s, 4)
        remote(
            a_send.at[0], a_recv.at[from_mate], sem_a_send.at[s - 1], sem_a_recv.at[s - 1], me, after
        ).wait_recv()
    totals = [a_recv[0]]
    for r in range(1, 4):
        totals.append(totals[-1] + a_recv[r])
    b_send[...] = totals[-1]
    b_copies = [
        remote(
            b_send,
            b_recv.at[s - 1],
            sem_b_send.at[s - 1],
            sem_b_recv.at[s - 1],
            me,
            lax.rem(team + s, teams) * 4 + seat,
        )
        for s in range(1, teams)
    ]
    for copy in b_copies:
        copy.start()
    base = jnp.zeros_like(totals[0])
    for s, copy in enumerate(b_copies, 1):
        copy.wait_recv()
        base = base + jnp.where(team >= s, b_recv[s - 1], 0.0)

    in_low = lax.broadcasted_iota(jnp.int32, (videos, lanes), 1) < quarter
    for r in range(4):
        total = base + totals[r]
        value = total[:videos] / column(total[videos : videos + 1, :videos])
        swapped = jnp.concatenate([value[:, quarter:], value[:, :quarter]], axis=1)
        var = value - swapped * swapped
        c_send[r] = jnp.where(in_low, value, lax.rsqrt(var + 1e-05) * my_gain)
    c_copies = mates(c_send, c_recv, sem_s_send, sem_s_recv)
    for copy in c_copies:
        copy.start()
    c_recv[seat] = c_send[seat]
    for s in range(1, 4):
        from_mate = lax.rem(seat + 4 - s, 4)
        remote(
            c_send.at[0], c_recv.at[from_mate], sem_s_send.at[s - 1], sem_s_recv.at[s - 1], me, after
        ).wait_recv()
    mean_v[...] = jnp.concatenate([c_recv[r][:, :quarter] for r in range(4)], axis=1)
    scale_v[...] = jnp.concatenate([c_recv[r][:, quarter:] for r in range(4)], axis=1)

    def exchange(i):
        stage[i, me, 0] = enc[i][pack_s[0, 2 * me]]
        stage[i, me, 1] = enc[i][pack_s[0, 2 * me + 1]]
        recv[i][me] = stage[i, me]

        @pl.loop(1, loads)
        def _(s):
            to = lax.rem(me + s, loads)
            stage[i, to, 0] = enc[i][pack_s[0, 2 * to]]
            stage[i, to, 1] = enc[i][pack_s[0, 2 * to + 1]]
            remote(stage.at[i, to], recv[i].at[me], sem_x_send.at[i], sem_x_recv.at[i], to, t).start()

    def all_of(i):
        sent = pl.ds(0, loads - 1)
        return remote(stage.at[i, sent], recv[i].at[sent], sem_x_send.at[i], sem_x_recv.at[i], me, after)

    @pl.loop(0, videos // group)
    def _(g):
        at = pl.ds(pl.multiple_of(g * group, group), group)
        place = pl.ds(pl.multiple_of(g * rows, rows), rows)
        mean = mean_v[at][:, None, :]
        scale = scale_v[at][:, None, :]
        taps = []
        for j in range(4):
            value = first[j, place].astype(F32).reshape(group, places, channels)
            value = ((value - mean) * scale).reshape(rows, channels).astype(BF16)
            first[j, place] = value
            taps.append(value)
        lhs = jnp.concatenate(taps[:3], axis=1)
        value = masked(dot(lhs, w2[...]) + bias[...], group_live(g, 2, lambda n: (n + 1) // 2))
        enc_1[at] = value.astype(BF16)

    exchange(1)

    @pl.loop(0, videos // group)
    def _(g):
        place = pl.ds(pl.multiple_of(g * rows, rows), rows)
        normed = [first[j, place].astype(F32).reshape(group, places, channels) for j in range(4)]
        ends = []
        for k in range(2):
            pieces = []
            for i in range(group):
                n = (cnt_s[0, g * group + i] + 1) // 2
                pieces.append(
                    jnp.where(
                        n == 2,
                        normed[k][i : i + 1],
                        jnp.where(n == 3, normed[k + 1][i : i + 1], normed[k + 2][i : i + 1]),
                    )
                )
            ends.append(jnp.concatenate(pieces, axis=0).reshape(rows, channels).astype(BF16))
        t2_send[place] = dot(jnp.concatenate(ends, axis=1), w2[: 2 * channels]).astype(BF16)

    t2 = remote(t2_send, t2_recv, sem_t.at[0], sem_t.at[1], me, after)
    t2.start()
    t2.wait_recv()

    @pl.loop(0, videos // group)
    def _(g):
        at = pl.ds(g * group, group)
        place = pl.ds(pl.multiple_of(g * rows, rows), rows)
        part = jnp.where(t > 0, t2_recv[place].astype(F32), 0.0)
        value = part + dot(first[0, place], w2[2 * channels :]) + bias[...]
        enc_0[at] = value.reshape(group, places, channels).astype(BF16)

    exchange(0)

    others = pl.ds(0, loads - 1)
    remote(d_recv.at[others], d_recv.at[others], sem_t.at[2], sem_t.at[3], me, after).wait()
    known = d_recv[...][:, 0, :]
    loader = lax.broadcasted_iota(jnp.int32, known.shape, 0)
    for i in range(pairs):
        table[i] = jnp.clip(jnp.sum(jnp.where(known == me * videos + 2 * i, loader, 0)), 0, loads - 1)

    for g in range(videos // group):
        context(g).wait_send()
    for copy in [t2] + a_copies + b_copies + c_copies:
        copy.wait_send()

    for i in (1, 0):
        all_of(i).wait_recv()

        @pl.loop(0, pairs)
        def _(q):
            out[2 * q, i] = recv[i][table[q], 0]
            out[2 * q + 1, i] = recv[i][table[q], 1]

        all_of(i).wait_send()


def body(loads, spans, frames, counts, dest, first_weight, second_weight, gain, bias):
    videos, length, places, channels = frames.shape[1:]
    group = min(16, videos)
    rows = videos * places
    vmem = pl.BlockSpec(memory_space=pltpu.VMEM)
    hbm = pl.BlockSpec(memory_space=pltpu.HBM)
    message = (videos + 8, 128)
    result = pl.pallas_call(
        functools.partial(kernel, loads, spans, group),
        out_shape=jax.ShapeDtypeStruct((videos, 2, places, channels), BF16),
        in_specs=[hbm] * 7,
        out_specs=vmem,
        scratch_shapes=[
            pltpu.SMEM((1, videos), jnp.int32),
            pltpu.VMEM((1, videos), jnp.int32),
            pltpu.VMEM((1, videos), jnp.int32),
            pltpu.VMEM((videos, length, places, channels), BF16),
            pltpu.VMEM((3 * channels, channels), BF16),
            pltpu.VMEM((3 * channels, channels), BF16),
            pltpu.VMEM((1, channels), F32),
            pltpu.VMEM((1, channels), F32),
            pltpu.VMEM((1, 128), jnp.int32),
            pltpu.SMEM((1, 128), jnp.int32),
            pltpu.VMEM((2, videos, places, channels), BF16),
            pltpu.VMEM((rows, channels), BF16),
            pltpu.VMEM((rows, channels), BF16),
            pltpu.VMEM((rows, channels), BF16),
            pltpu.VMEM((rows, channels), BF16),
            pltpu.VMEM((4, rows, channels), BF16),
            pltpu.VMEM((videos, 8, channels), F32),
            pltpu.VMEM((videos, 8, channels), F32),
            pltpu.VMEM((4,) + message, F32),
            pltpu.VMEM((4,) + message, F32),
            pltpu.VMEM(message, F32),
            pltpu.VMEM((spans // 4 - 1,) + message, F32),
            pltpu.VMEM((4, videos, 128), F32),
            pltpu.VMEM((4, videos, 128), F32),
            pltpu.VMEM((videos, channels), F32),
            pltpu.VMEM((videos, channels), F32),
            pltpu.VMEM((videos, places, channels), BF16),
            pltpu.VMEM((videos, places, channels), BF16),
            pltpu.VMEM((2, loads, 2, places, channels), BF16),
            pltpu.VMEM((loads, 2, places, channels), BF16),
            pltpu.VMEM((loads, 2, places, channels), BF16),
            pltpu.VMEM((8, 128), jnp.int32),
            pltpu.VMEM((loads, 8, 128), jnp.int32),
            pltpu.SMEM((videos // 2,), jnp.int32),
            pltpu.SemaphoreType.DMA((12,)),
            pltpu.SemaphoreType.DMA((4,)),
            pltpu.SemaphoreType.DMA((videos // group,)),
            pltpu.SemaphoreType.DMA((videos // group,)),
            pltpu.SemaphoreType.DMA((3,)),
            pltpu.SemaphoreType.DMA((3,)),
            pltpu.SemaphoreType.DMA((spans // 4 - 1,)),
            pltpu.SemaphoreType.DMA((spans // 4 - 1,)),
            pltpu.SemaphoreType.DMA((3,)),
            pltpu.SemaphoreType.DMA((3,)),
            pltpu.SemaphoreType.DMA((2,)),
            pltpu.SemaphoreType.DMA((2,)),
        ],
        compiler_params=pltpu.CompilerParams(
            collective_id=0, has_side_effects=True, vmem_limit_bytes=63 * 1024 * 1024
        ),
    )(
        counts,
        dest.reshape(1, videos),
        frames[0],
        first_weight.reshape(3 * channels, channels),
        second_weight.reshape(3 * channels, channels),
        gain.reshape(1, channels),
        bias.reshape(1, channels),
    )
    return result[None]


def solution(mesh):
    loads, spans = mesh.shape["load"], mesh.shape["tm"]
    return jax.shard_map(
        functools.partial(body, loads, spans),
        mesh=mesh,
        in_specs=(
            P("tm", "load", None, None, None),
            P("tm", "load"),
            P("load"),
            P(),
            P(),
            P(),
            P(),
        ),
        out_specs=P("tm", "load", None, None, None),
        check_vma=False,
    )
```

```python
import functools

import jax
import jax.numpy as jnp
from jax import lax
from jax.experimental import pallas as pl
from jax.experimental.pallas import tpu as pltpu
from jax.sharding import PartitionSpec as P

F32 = jnp.float32
BF16 = jnp.bfloat16
MESH = pl.DeviceIdType.MESH


def flat(x):
    videos, places, channels = x.shape
    return x.astype(F32).reshape(videos * places, channels).astype(BF16)


def dot(a, b):
    return jnp.dot(a, b, preferred_element_type=F32)


def silu(x):
    h = 0.5 * x
    return h + h * jnp.tanh(h)


def kernel(
    loads,
    spans,
    group,
    counts_hbm,
    dest_hbm,
    frames_hbm,
    w1_hbm,
    w2_hbm,
    gain_hbm,
    bias_hbm,
    out,
    cnt_s,
    cnt_v,
    dest_v,
    frames,
    w1,
    w2,
    gain,
    bias,
    pack_v,
    pack_s,
    tail,
    t1_send,
    t1_recv,
    t2_send,
    t2_recv,
    first,
    acc1,
    acc2,
    a_send,
    a_recv,
    b_send,
    b_recv,
    c_send,
    c_recv,
    mean_v,
    scale_v,
    enc_0,
    enc_1,
    stage,
    recv_0,
    recv_1,
    d_send,
    d_recv,
    table,
    sem_in,
    sem_t,
    sem_c_send,
    sem_c_recv,
    sem_a_send,
    sem_a_recv,
    sem_ready,
    sem_b,
    sem_s_send,
    sem_s_recv,
    sem_x_send,
    sem_x_recv,
):
    videos, places, channels = frames.shape[0], frames.shape[2], frames.shape[3]
    length = frames.shape[1]
    quarter = channels // 4
    rows = group * places
    pairs = videos // 2
    me = lax.axis_index("load")
    t = lax.axis_index("tm")
    team = t // 4
    seat = t % 4
    after = lax.rem(t + 1, spans)
    beyond = lax.rem(t + jnp.where(seat == 0, spans - 1, 1), spans)
    has_before, has_after = t > 0, t < spans - 1
    team_before, team_after = t >= 4, t < spans - 4
    edge = jnp.logical_or(jnp.logical_and(seat == 0, has_before), jnp.logical_and(seat == 3, has_after))

    pieces = 4
    part = videos // pieces
    fetches = [
        pltpu.make_async_copy(a, b, sem_in.at[i])
        for i, (a, b) in enumerate(
            [(counts_hbm, cnt_s), (counts_hbm, cnt_v), (dest_hbm, dest_v)]
            + [(frames_hbm.at[pl.ds(q * part, part)], frames.at[pl.ds(q * part, part)]) for q in range(pieces)]
            + [(w1_hbm, w1), (w2_hbm, w2), (gain_hbm, gain), (bias_hbm, bias)]
        )
    ]
    for fetch in fetches:
        fetch.start()

    enc = (enc_0, enc_1)
    recv = (recv_0, recv_1)
    barrier = pltpu.get_barrier_semaphore()

    def greet(load, place):
        pl.semaphore_signal(barrier, inc=1, device_id=(load, place), device_id_type=MESH)

    @pl.when(edge)
    def _():
        greet(me, beyond)

    for s in range(1, 4):
        greet(me, team * 4 + lax.rem(seat + s, 4))

    @pl.when(team_after)
    def _():
        greet(me, lax.rem(t + 4, spans))

    @pl.loop(1, loads)
    def _(s):
        greet(lax.rem(me + s, loads), t)

    for fetch in fetches[:-3]:
        fetch.wait()

    @pl.loop(0, videos)
    def _(v):
        tail[0, v] = frames[v, jnp.clip(cnt_s[0, v] - 2, 0, length - 1)]
        tail[1, v] = frames[v, jnp.clip(cnt_s[0, v] - 1, 0, length - 1)]

    @pl.loop(0, videos // group)
    def _(g):
        at = pl.ds(g * group, group)
        lhs = jnp.concatenate([flat(tail[0, at]), flat(tail[1, at])], axis=1)
        t1_send[pl.ds(pl.multiple_of(g * rows, rows), rows)] = dot(lhs, w1[: 2 * channels]).astype(BF16)

    lanes = 128
    row = jnp.pad(dest_v[...], ((0, 7), (0, lanes - videos)), constant_values=-1)
    d_send[...] = row

    pl.semaphore_wait(barrier, 3 + (loads - 1) + jnp.where(edge, 1, 0) + jnp.where(team_before, 1, 0))

    @pl.when(team_before)
    def _():
        pl.semaphore_signal(
            sem_ready, inc=1, device_id=(me, lax.rem(t + spans - 4, spans)), device_id_type=MESH
        )

    def remote(src, dst, ss, rs, load, place):
        return pltpu.make_async_remote_copy(
            src_ref=src, dst_ref=dst, send_sem=ss, recv_sem=rs, device_id=(load, place), device_id_type=MESH
        )

    def context(g):
        place = pl.ds(pl.multiple_of(g * rows, rows), rows)
        return remote(t1_send.at[place], t1_recv.at[place], sem_c_send.at[g], sem_c_recv.at[g], me, after)

    @pl.when(has_after)
    def _():
        for g in range(videos // group):
            context(g).start()

    d_recv[me] = row

    def column(values):
        r = lax.broadcasted_iota(jnp.int32, (videos, videos), 0)
        c = lax.broadcasted_iota(jnp.int32, (videos, videos), 1)
        return jnp.sum(jnp.where(r == c, values, 0), axis=1, keepdims=True)

    for fetch in fetches[-3:]:
        fetch.wait()
    counts_row = cnt_v[...]

    place_of = column(dest_v[...])
    place_of = place_of // videos * 2 + place_of % 2
    lane = lax.broadcasted_iota(jnp.int32, (videos, 128), 1)
    video = lax.broadcasted_iota(jnp.int32, (videos, 128), 0)
    pack_v[...] = jnp.clip(jnp.sum(jnp.where(place_of == lane, video, 0), axis=0, keepdims=True), 0, videos - 1)
    to_scalars = pltpu.make_async_copy(pack_v, pack_s, sem_in.at[len(fetches)])
    to_scalars.start()

    def add_sums(g, at, values, fresh):
        tiles = values.reshape(group, places // 8, 8, channels)
        s1 = jnp.sum(tiles, axis=1)
        s2 = jnp.sum(tiles * tiles, axis=1)
        if fresh:
            acc1[at] = s1
            acc2[at] = s2
        else:
            acc1[at] += s1
            acc2[at] += s2

    def group_live(g, step, limit_of):
        parts = [limit_of(cnt_s[0, g * group + i]) > step for i in range(group)]
        return parts

    def masked(value, flags):
        pieces = value.reshape(group, places, channels)
        return jnp.concatenate(
            [jnp.where(flags[i], pieces[i : i + 1], 0.0) for i in range(group)], axis=0
        )

    @pl.loop(0, videos // group)
    def _(g):
        at = pl.ds(g * group, group)
        place = pl.ds(pl.multiple_of(g * rows, rows), rows)
        for j in range(1, 4):
            lhs = jnp.concatenate([flat(frames[at, 2 * j - 2 + k]) for k in range(3)], axis=1)
            value = masked(silu(dot(lhs, w1[...])), group_live(g, 2 * j, lambda n: n))
            value = value.reshape(rows, channels).astype(BF16)
            first[j, place] = value
            add_sums(g, at, value.astype(F32), j == 1)

    @pl.loop(1, loads)
    def _(s):
        remote(d_send, d_recv.at[me], sem_t.at[2], sem_t.at[3], lax.rem(me + s, loads), t).start()

    to_scalars.wait()

    @pl.loop(0, videos // group)
    def _(g):
        at = pl.ds(g * group, group)
        place = pl.ds(pl.multiple_of(g * rows, rows), rows)

        @pl.when(has_before)
        def _():
            context(g).wait_recv()

        part = jnp.where(has_before, t1_recv[place].astype(F32), 0.0)
        value = silu(part + dot(flat(frames[at, 0]), w1[2 * channels :])).astype(BF16)
        first[0, place] = value
        add_sums(g, at, value.astype(F32), False)

    s1 = jnp.sum(acc1[...], axis=1)
    s2 = jnp.sum(acc2[...], axis=1)
    num = (((counts_row + 1) // 2) * places).astype(F32)
    num = jnp.pad(num, ((0, 7), (0, lanes - videos)))

    def parts(x):
        return [x[:, r * quarter : (r + 1) * quarter] for r in range(4)]

    for r, (p1, p2) in enumerate(zip(parts(s1), parts(s2))):
        a_send[r] = jnp.concatenate([jnp.concatenate([p1, p2], axis=1), num], axis=0)

    def mates(source, target, ss, rs):
        made = []
        for s in range(1, 4):
            mate = lax.rem(seat + s, 4)
            made.append(
                remote(source.at[mate], target.at[seat], ss.at[s - 1], rs.at[s - 1], me, team * 4 + mate)
            )
        return made

    a_copies = mates(a_send, a_recv, sem_a_send, sem_a_recv)
    for copy in a_copies:
        copy.start()
    a_recv[seat] = a_send[seat]
    my_gain = sum(jnp.where(seat == r, g, 0.0) for r, g in enumerate(parts(gain[...])))
    my_gain = jnp.concatenate([my_gain, my_gain], axis=1)
    for s in range(1, 4):
        from_mate = lax.rem(seat + 4 - s, 4)
        remote(
            a_send.at[0], a_recv.at[from_mate], sem_a_send.at[s - 1], sem_a_recv.at[s - 1], me, after
        ).wait_recv()
    totals = [a_recv[0]]
    for r in range(1, 4):
        totals.append(totals[-1] + a_recv[r])
    b_copy = remote(b_send, b_recv, sem_b.at[0], sem_b.at[1], me, lax.rem(t + 4, spans))

    @pl.when(team_before)
    def _():
        b_copy.wait_recv()

    base = jnp.where(team_before, b_recv[...], 0.0)
    b_send[...] = base + totals[-1]

    @pl.when(team_after)
    def _():
        pl.semaphore_wait(sem_ready, 1)
        b_copy.start()

    in_low = lax.broadcasted_iota(jnp.int32, (videos, lanes), 1) < quarter
    for r in range(4):
        total = base + totals[r]
        value = total[:videos] / column(total[videos : videos + 1, :videos])
        swapped = jnp.concatenate([value[:, quarter:], value[:, :quarter]], axis=1)
        var = value - swapped * swapped
        c_send[r] = jnp.where(in_low, value, lax.rsqrt(var + 1e-05) * my_gain)
    c_copies = mates(c_send, c_recv, sem_s_send, sem_s_recv)
    for copy in c_copies:
        copy.start()
    c_recv[seat] = c_send[seat]
    for s in range(1, 4):
        from_mate = lax.rem(seat + 4 - s, 4)
        remote(
            c_send.at[0], c_recv.at[from_mate], sem_s_send.at[s - 1], sem_s_recv.at[s - 1], me, after
        ).wait_recv()
    mean_v[...] = jnp.concatenate([c_recv[r][:, :quarter] for r in range(4)], axis=1)
    scale_v[...] = jnp.concatenate([c_recv[r][:, quarter:] for r in range(4)], axis=1)

    def exchange(i):
        stage[i, me, 0] = enc[i][pack_s[0, 2 * me]]
        stage[i, me, 1] = enc[i][pack_s[0, 2 * me + 1]]
        recv[i][me] = stage[i, me]

        @pl.loop(1, loads)
        def _(s):
            to = lax.rem(me + s, loads)
            stage[i, to, 0] = enc[i][pack_s[0, 2 * to]]
            stage[i, to, 1] = enc[i][pack_s[0, 2 * to + 1]]
            remote(stage.at[i, to], recv[i].at[me], sem_x_send.at[i], sem_x_recv.at[i], to, t).start()

    def all_of(i):
        sent = pl.ds(0, loads - 1)
        return remote(stage.at[i, sent], recv[i].at[sent], sem_x_send.at[i], sem_x_recv.at[i], me, after)

    @pl.loop(0, videos // group)
    def _(g):
        at = pl.ds(pl.multiple_of(g * group, group), group)
        place = pl.ds(pl.multiple_of(g * rows, rows), rows)
        mean = mean_v[at][:, None, :]
        scale = scale_v[at][:, None, :]
        taps = []
        for j in range(4):
            value = first[j, place].astype(F32).reshape(group, places, channels)
            value = ((value - mean) * scale).reshape(rows, channels).astype(BF16)
            first[j, place] = value
            taps.append(value)
        lhs = jnp.concatenate(taps[:3], axis=1)
        value = masked(dot(lhs, w2[...]) + bias[...], group_live(g, 2, lambda n: (n + 1) // 2))
        enc_1[at] = value.astype(BF16)

    exchange(1)

    @pl.loop(0, videos // group)
    def _(g):
        place = pl.ds(pl.multiple_of(g * rows, rows), rows)
        normed = [first[j, place].astype(F32).reshape(group, places, channels) for j in range(4)]
        ends = []
        for k in range(2):
            pieces = []
            for i in range(group):
                n = (cnt_s[0, g * group + i] + 1) // 2
                pieces.append(
                    jnp.where(
                        n == 2,
                        normed[k][i : i + 1],
                        jnp.where(n == 3, normed[k + 1][i : i + 1], normed[k + 2][i : i + 1]),
                    )
                )
            ends.append(jnp.concatenate(pieces, axis=0).reshape(rows, channels).astype(BF16))
        t2_send[place] = dot(jnp.concatenate(ends, axis=1), w2[: 2 * channels]).astype(BF16)

    t2 = remote(t2_send, t2_recv, sem_t.at[0], sem_t.at[1], me, after)

    @pl.when(has_after)
    def _():
        t2.start()


    @pl.when(has_before)
    def _():
        t2.wait_recv()

    @pl.loop(0, videos // group)
    def _(g):
        at = pl.ds(g * group, group)
        place = pl.ds(pl.multiple_of(g * rows, rows), rows)
        part = jnp.where(has_before, t2_recv[place].astype(F32), 0.0)
        value = part + dot(first[0, place], w2[2 * channels :]) + bias[...]
        enc_0[at] = value.reshape(group, places, channels).astype(BF16)

    exchange(0)

    others = pl.ds(0, loads - 1)
    remote(d_recv.at[others], d_recv.at[others], sem_t.at[2], sem_t.at[3], me, after).wait()
    known = d_recv[...][:, 0, :]
    loader = lax.broadcasted_iota(jnp.int32, known.shape, 0)
    for i in range(pairs):
        table[i] = jnp.clip(jnp.sum(jnp.where(known == me * videos + 2 * i, loader, 0)), 0, loads - 1)

    for copy in a_copies + c_copies:
        copy.wait_send()

    @pl.when(has_after)
    def _():
        for g in range(videos // group):
            context(g).wait_send()
        t2.wait_send()

    @pl.when(team_after)
    def _():
        b_copy.wait_send()


    for i in (1, 0):
        all_of(i).wait_recv()

        @pl.loop(0, pairs)
        def _(q):
            out[2 * q, i] = recv[i][table[q], 0]
            out[2 * q + 1, i] = recv[i][table[q], 1]

        all_of(i).wait_send()


def body(loads, spans, frames, counts, dest, first_weight, second_weight, gain, bias):
    videos, length, places, channels = frames.shape[1:]
    group = min(16, videos)
    rows = videos * places
    vmem = pl.BlockSpec(memory_space=pltpu.VMEM)
    hbm = pl.BlockSpec(memory_space=pltpu.HBM)
    message = (videos + 8, 128)
    result = pl.pallas_call(
        functools.partial(kernel, loads, spans, group),
        out_shape=jax.ShapeDtypeStruct((videos, 2, places, channels), BF16),
        in_specs=[hbm] * 7,
        out_specs=vmem,
        scratch_shapes=[
            pltpu.SMEM((1, videos), jnp.int32),
            pltpu.VMEM((1, videos), jnp.int32),
            pltpu.VMEM((1, videos), jnp.int32),
            pltpu.VMEM((videos, length, places, channels), BF16),
            pltpu.VMEM((3 * channels, channels), BF16),
            pltpu.VMEM((3 * channels, channels), BF16),
            pltpu.VMEM((1, channels), F32),
            pltpu.VMEM((1, channels), F32),
            pltpu.VMEM((1, 128), jnp.int32),
            pltpu.SMEM((1, 128), jnp.int32),
            pltpu.VMEM((2, videos, places, channels), BF16),
            pltpu.VMEM((rows, channels), BF16),
            pltpu.VMEM((rows, channels), BF16),
            pltpu.VMEM((rows, channels), BF16),
            pltpu.VMEM((rows, channels), BF16),
            pltpu.VMEM((4, rows, channels), BF16),
            pltpu.VMEM((videos, 8, channels), F32),
            pltpu.VMEM((videos, 8, channels), F32),
            pltpu.VMEM((4,) + message, F32),
            pltpu.VMEM((4,) + message, F32),
            pltpu.VMEM(message, F32),
            pltpu.VMEM(message, F32),
            pltpu.VMEM((4, videos, 128), F32),
            pltpu.VMEM((4, videos, 128), F32),
            pltpu.VMEM((videos, channels), F32),
            pltpu.VMEM((videos, channels), F32),
            pltpu.VMEM((videos, places, channels), BF16),
            pltpu.VMEM((videos, places, channels), BF16),
            pltpu.VMEM((2, loads, 2, places, channels), BF16),
            pltpu.VMEM((loads, 2, places, channels), BF16),
            pltpu.VMEM((loads, 2, places, channels), BF16),
            pltpu.VMEM((8, 128), jnp.int32),
            pltpu.VMEM((loads, 8, 128), jnp.int32),
            pltpu.SMEM((videos // 2,), jnp.int32),
            pltpu.SemaphoreType.DMA((12,)),
            pltpu.SemaphoreType.DMA((4,)),
            pltpu.SemaphoreType.DMA((videos // group,)),
            pltpu.SemaphoreType.DMA((videos // group,)),
            pltpu.SemaphoreType.DMA((3,)),
            pltpu.SemaphoreType.DMA((3,)),
            pltpu.SemaphoreType.REGULAR,
            pltpu.SemaphoreType.DMA((2,)),
            pltpu.SemaphoreType.DMA((3,)),
            pltpu.SemaphoreType.DMA((3,)),
            pltpu.SemaphoreType.DMA((2,)),
            pltpu.SemaphoreType.DMA((2,)),
        ],
        compiler_params=pltpu.CompilerParams(
            collective_id=0, has_side_effects=True, vmem_limit_bytes=63 * 1024 * 1024
        ),
    )(
        counts,
        dest.reshape(1, videos),
        frames[0],
        first_weight.reshape(3 * channels, channels),
        second_weight.reshape(3 * channels, channels),
        gain.reshape(1, channels),
        bias.reshape(1, channels),
    )
    return result[None]


def solution(mesh):
    loads, spans = mesh.shape["load"], mesh.shape["tm"]
    return jax.shard_map(
        functools.partial(body, loads, spans),
        mesh=mesh,
        in_specs=(
            P("tm", "load", None, None, None),
            P("tm", "load"),
            P("load"),
            P(),
            P(),
            P(),
            P(),
        ),
        out_specs=P("tm", "load", None, None, None),
        check_vma=False,
    )
```

```python
import functools

import jax
import jax.numpy as jnp
from jax import lax
from jax.experimental import pallas as pl
from jax.experimental.pallas import tpu as pltpu
from jax.sharding import PartitionSpec as P

F32 = jnp.float32
BF16 = jnp.bfloat16
MESH = pl.DeviceIdType.MESH


def flat(x):
    videos, places, channels = x.shape
    return x.astype(F32).reshape(videos * places, channels).astype(BF16)


def dot(a, b):
    return jnp.dot(a, b, preferred_element_type=F32)


def silu(x):
    h = 0.5 * x
    return h + h * jnp.tanh(h)


def kernel(
    loads,
    spans,
    group,
    counts_hbm,
    dest_hbm,
    frames_hbm,
    w1_hbm,
    w2_hbm,
    gain_hbm,
    bias_hbm,
    out,
    cnt_s,
    cnt_v,
    dest_v,
    frames,
    w1,
    w2,
    gain,
    bias,
    pack_v,
    pack_s,
    tail,
    t1_send,
    t1_recv,
    t2_send,
    t2_recv,
    first,
    acc1,
    acc2,
    a_send,
    a_recv,
    b_send,
    b_recv,
    c_send,
    c_recv,
    mean_v,
    scale_v,
    enc_0,
    enc_1,
    stage,
    recv_0,
    recv_1,
    d_send,
    d_recv,
    table,
    sem_in,
    sem_t,
    sem_c_send,
    sem_c_recv,
    sem_a_send,
    sem_a_recv,
    sem_ready,
    sem_b,
    sem_s_send,
    sem_s_recv,
    sem_x_send,
    sem_x_recv,
):
    videos, places, channels = frames.shape[0], frames.shape[2], frames.shape[3]
    length = frames.shape[1]
    quarter = channels // 4
    rows = group * places
    pairs = videos // 2
    me = lax.axis_index("load")
    t = lax.axis_index("tm")
    team = t // 4
    seat = t % 4
    after = lax.rem(t + 1, spans)
    beyond = lax.rem(t + jnp.where(seat == 0, spans - 1, 1), spans)
    has_before, has_after = t > 0, t < spans - 1
    team_before, team_after = t >= 4, t < spans - 4
    edge = jnp.logical_or(jnp.logical_and(seat == 0, has_before), jnp.logical_and(seat == 3, has_after))

    pieces = 4
    part = videos // pieces
    fetches = [
        pltpu.make_async_copy(a, b, sem_in.at[i])
        for i, (a, b) in enumerate(
            [(counts_hbm, cnt_s), (counts_hbm, cnt_v), (dest_hbm, dest_v)]
            + [(frames_hbm.at[pl.ds(q * part, part)], frames.at[pl.ds(q * part, part)]) for q in range(pieces)]
            + [(w1_hbm, w1), (w2_hbm, w2), (gain_hbm, gain), (bias_hbm, bias)]
        )
    ]
    for fetch in fetches:
        fetch.start()

    enc = (enc_0, enc_1)
    recv = (recv_0, recv_1)
    barrier = pltpu.get_barrier_semaphore()

    def greet(load, place):
        pl.semaphore_signal(barrier, inc=1, device_id=(load, place), device_id_type=MESH)

    @pl.when(edge)
    def _():
        greet(me, beyond)

    for s in range(1, 4):
        greet(me, team * 4 + lax.rem(seat + s, 4))

    @pl.when(team_after)
    def _():
        greet(me, lax.rem(t + 4, spans))

    @pl.loop(1, loads)
    def _(s):
        greet(lax.rem(me + s, loads), t)

    for fetch in fetches[:-3]:
        fetch.wait()

    lanes = 128
    row = jnp.pad(dest_v[...], ((0, 7), (0, lanes - videos)), constant_values=-1)
    d_send[...] = row

    pl.semaphore_wait(barrier, 3 + (loads - 1) + jnp.where(edge, 1, 0) + jnp.where(team_before, 1, 0))

    @pl.when(team_before)
    def _():
        pl.semaphore_signal(
            sem_ready, inc=1, device_id=(me, lax.rem(t + spans - 4, spans)), device_id_type=MESH
        )

    def remote(src, dst, ss, rs, load, place):
        return pltpu.make_async_remote_copy(
            src_ref=src, dst_ref=dst, send_sem=ss, recv_sem=rs, device_id=(load, place), device_id_type=MESH
        )

    few = min(8, videos)
    few_rows = few * places

    def context(q):
        place = pl.ds(pl.multiple_of(q * few_rows, few_rows), few_rows)
        return remote(t1_send.at[place], t1_recv.at[place], sem_c_send.at[q], sem_c_recv.at[q], me, after)

    @pl.loop(0, videos // few)
    def _(q):
        for i in range(few):
            v = q * few + i
            tail[0, v] = frames[v, jnp.clip(cnt_s[0, v] - 2, 0, length - 1)]
            tail[1, v] = frames[v, jnp.clip(cnt_s[0, v] - 1, 0, length - 1)]
        at = pl.ds(q * few, few)
        lhs = jnp.concatenate([flat(tail[0, at]), flat(tail[1, at])], axis=1)
        t1_send[pl.ds(pl.multiple_of(q * few_rows, few_rows), few_rows)] = dot(lhs, w1[: 2 * channels]).astype(BF16)

        @pl.when(has_after)
        def _():
            context(q).start()

    d_recv[me] = row

    def column(values):
        r = lax.broadcasted_iota(jnp.int32, (videos, videos), 0)
        c = lax.broadcasted_iota(jnp.int32, (videos, videos), 1)
        return jnp.sum(jnp.where(r == c, values, 0), axis=1, keepdims=True)

    for fetch in fetches[-3:]:
        fetch.wait()
    counts_row = cnt_v[...]

    def add_sums(at, values, fresh):
        tiles = values.reshape(-1, places // 8, 8, channels)
        s1 = jnp.sum(tiles, axis=1)
        s2 = jnp.sum(tiles * tiles, axis=1)
        if fresh:
            acc1[at] = s1
            acc2[at] = s2
        else:
            acc1[at] += s1
            acc2[at] += s2

    def group_live(g, step, limit_of):
        parts = [limit_of(cnt_s[0, g * group + i]) > step for i in range(group)]
        return parts

    def masked(value, flags):
        pieces = value.reshape(group, places, channels)
        return jnp.concatenate(
            [jnp.where(flags[i], pieces[i : i + 1], 0.0) for i in range(group)], axis=0
        )

    @pl.loop(0, videos // group)
    def _(g):
        at = pl.ds(g * group, group)
        place = pl.ds(pl.multiple_of(g * rows, rows), rows)
        for j in range(1, 4):
            lhs = jnp.concatenate([flat(frames[at, 2 * j - 2 + k]) for k in range(3)], axis=1)
            value = masked(silu(dot(lhs, w1[...])), group_live(g, 2 * j, lambda n: n))
            value = value.reshape(rows, channels).astype(BF16)
            first[j, place] = value
            add_sums(at, value.astype(F32), j == 1)

    @pl.loop(0, videos // few)
    def _(q):
        at = pl.ds(q * few, few)
        place = pl.ds(pl.multiple_of(q * few_rows, few_rows), few_rows)

        @pl.when(has_before)
        def _():
            context(q).wait_recv()

        part = jnp.where(has_before, t1_recv[place].astype(F32), 0.0)
        value = silu(part + dot(flat(frames[at, 0]), w1[2 * channels :])).astype(BF16)
        first[0, place] = value
        add_sums(at, value.astype(F32), False)

    s1 = jnp.sum(acc1[...], axis=1)
    s2 = jnp.sum(acc2[...], axis=1)
    num = (((counts_row + 1) // 2) * places).astype(F32)
    num = jnp.pad(num, ((0, 7), (0, lanes - videos)))

    def parts(x):
        return [x[:, r * quarter : (r + 1) * quarter] for r in range(4)]

    for r, (p1, p2) in enumerate(zip(parts(s1), parts(s2))):
        a_send[r] = jnp.concatenate([jnp.concatenate([p1, p2], axis=1), num], axis=0)

    def mates(source, target, ss, rs):
        made = []
        for s in range(1, 4):
            mate = lax.rem(seat + s, 4)
            made.append(
                remote(source.at[mate], target.at[seat], ss.at[s - 1], rs.at[s - 1], me, team * 4 + mate)
            )
        return made

    a_copies = mates(a_send, a_recv, sem_a_send, sem_a_recv)
    for copy in a_copies:
        copy.start()
    a_recv[seat] = a_send[seat]

    place_of = column(dest_v[...])
    place_of = place_of // videos * 2 + place_of % 2
    lane = lax.broadcasted_iota(jnp.int32, (videos, 128), 1)
    video = lax.broadcasted_iota(jnp.int32, (videos, 128), 0)
    pack_v[...] = jnp.clip(jnp.sum(jnp.where(place_of == lane, video, 0), axis=0, keepdims=True), 0, videos - 1)
    to_scalars = pltpu.make_async_copy(pack_v, pack_s, sem_in.at[len(fetches)])
    to_scalars.start()

    my_gain = sum(jnp.where(seat == r, g, 0.0) for r, g in enumerate(parts(gain[...])))
    my_gain = jnp.concatenate([my_gain, my_gain], axis=1)
    for s in range(1, 4):
        from_mate = lax.rem(seat + 4 - s, 4)
        remote(
            a_send.at[0], a_recv.at[from_mate], sem_a_send.at[s - 1], sem_a_recv.at[s - 1], me, after
        ).wait_recv()
    totals = [a_recv[0]]
    for r in range(1, 4):
        totals.append(totals[-1] + a_recv[r])
    b_copy = remote(b_send, b_recv, sem_b.at[0], sem_b.at[1], me, lax.rem(t + 4, spans))

    @pl.when(team_before)
    def _():
        b_copy.wait_recv()

    base = jnp.where(team_before, b_recv[...], 0.0)
    b_send[...] = base + totals[-1]

    @pl.when(team_after)
    def _():
        pl.semaphore_wait(sem_ready, 1)
        b_copy.start()

    in_low = lax.broadcasted_iota(jnp.int32, (videos, lanes), 1) < quarter
    for r in range(4):
        total = base + totals[r]
        value = total[:videos] / column(total[videos : videos + 1, :videos])
        swapped = jnp.concatenate([value[:, quarter:], value[:, :quarter]], axis=1)
        var = value - swapped * swapped
        c_send[r] = jnp.where(in_low, value, lax.rsqrt(var + 1e-05) * my_gain)
    c_copies = mates(c_send, c_recv, sem_s_send, sem_s_recv)
    for copy in c_copies:
        copy.start()
    c_recv[seat] = c_send[seat]
    for s in range(1, 4):
        from_mate = lax.rem(seat + 4 - s, 4)
        remote(
            c_send.at[0], c_recv.at[from_mate], sem_s_send.at[s - 1], sem_s_recv.at[s - 1], me, after
        ).wait_recv()
    mean_v[...] = jnp.concatenate([c_recv[r][:, :quarter] for r in range(4)], axis=1)
    scale_v[...] = jnp.concatenate([c_recv[r][:, quarter:] for r in range(4)], axis=1)

    def exchange(i):
        stage[i, me, 0] = enc[i][pack_s[0, 2 * me]]
        stage[i, me, 1] = enc[i][pack_s[0, 2 * me + 1]]
        recv[i][me] = stage[i, me]

        @pl.loop(1, loads)
        def _(s):
            to = lax.rem(me + s, loads)
            stage[i, to, 0] = enc[i][pack_s[0, 2 * to]]
            stage[i, to, 1] = enc[i][pack_s[0, 2 * to + 1]]
            remote(stage.at[i, to], recv[i].at[me], sem_x_send.at[i], sem_x_recv.at[i], to, t).start()

    def all_of(i):
        sent = pl.ds(0, loads - 1)
        return remote(stage.at[i, sent], recv[i].at[sent], sem_x_send.at[i], sem_x_recv.at[i], me, after)

    @pl.loop(0, videos // group)
    def _(g):
        at = pl.ds(pl.multiple_of(g * group, group), group)
        place = pl.ds(pl.multiple_of(g * rows, rows), rows)
        mean = mean_v[at][:, None, :]
        scale = scale_v[at][:, None, :]
        taps = []
        for j in range(3):
            value = first[j, place].astype(F32).reshape(group, places, channels)
            value = ((value - mean) * scale).reshape(rows, channels).astype(BF16)
            first[j, place] = value
            taps.append(value)
        lhs = jnp.concatenate(taps, axis=1)
        value = masked(dot(lhs, w2[...]) + bias[...], group_live(g, 2, lambda n: (n + 1) // 2))
        enc_1[at] = value.astype(BF16)

    to_scalars.wait()
    exchange(1)

    @pl.loop(1, loads)
    def _(s):
        remote(d_send, d_recv.at[me], sem_t.at[2], sem_t.at[3], lax.rem(me + s, loads), t).start()

    @pl.loop(0, videos // group)
    def _(g):
        place = pl.ds(pl.multiple_of(g * rows, rows), rows)
        at = pl.ds(pl.multiple_of(g * group, group), group)
        normed = [first[j, place].astype(F32).reshape(group, places, channels) for j in range(4)]
        normed[3] = (normed[3] - mean_v[at][:, None, :]) * scale_v[at][:, None, :]
        ends = []
        for k in range(2):
            pieces = []
            for i in range(group):
                n = (cnt_s[0, g * group + i] + 1) // 2
                pieces.append(
                    jnp.where(
                        n == 2,
                        normed[k][i : i + 1],
                        jnp.where(n == 3, normed[k + 1][i : i + 1], normed[k + 2][i : i + 1]),
                    )
                )
            ends.append(jnp.concatenate(pieces, axis=0).reshape(rows, channels).astype(BF16))
        t2_send[place] = dot(jnp.concatenate(ends, axis=1), w2[: 2 * channels]).astype(BF16)

    t2 = remote(t2_send, t2_recv, sem_t.at[0], sem_t.at[1], me, after)

    @pl.when(has_after)
    def _():
        t2.start()


    @pl.when(has_before)
    def _():
        t2.wait_recv()

    @pl.loop(0, videos // group)
    def _(g):
        at = pl.ds(g * group, group)
        place = pl.ds(pl.multiple_of(g * rows, rows), rows)
        part = jnp.where(has_before, t2_recv[place].astype(F32), 0.0)
        value = part + dot(first[0, place], w2[2 * channels :]) + bias[...]
        enc_0[at] = value.reshape(group, places, channels).astype(BF16)

    exchange(0)

    others = pl.ds(0, loads - 1)
    remote(d_recv.at[others], d_recv.at[others], sem_t.at[2], sem_t.at[3], me, after).wait()
    known = d_recv[...][:, 0, :]
    loader = lax.broadcasted_iota(jnp.int32, known.shape, 0)
    for i in range(pairs):
        table[i] = jnp.clip(jnp.sum(jnp.where(known == me * videos + 2 * i, loader, 0)), 0, loads - 1)

    for copy in a_copies + c_copies:
        copy.wait_send()

    @pl.when(has_after)
    def _():
        for q in range(videos // few):
            context(q).wait_send()
        t2.wait_send()

    @pl.when(team_after)
    def _():
        b_copy.wait_send()


    for i in (1, 0):
        all_of(i).wait_recv()

        @pl.loop(0, pairs)
        def _(q):
            out[2 * q, i] = recv[i][table[q], 0]
            out[2 * q + 1, i] = recv[i][table[q], 1]

        all_of(i).wait_send()


def body(loads, spans, frames, counts, dest, first_weight, second_weight, gain, bias):
    videos, length, places, channels = frames.shape[1:]
    group = min(16, videos)
    rows = videos * places
    vmem = pl.BlockSpec(memory_space=pltpu.VMEM)
    hbm = pl.BlockSpec(memory_space=pltpu.HBM)
    message = (videos + 8, 128)
    result = pl.pallas_call(
        functools.partial(kernel, loads, spans, group),
        out_shape=jax.ShapeDtypeStruct((videos, 2, places, channels), BF16),
        in_specs=[hbm] * 7,
        out_specs=vmem,
        scratch_shapes=[
            pltpu.SMEM((1, videos), jnp.int32),
            pltpu.VMEM((1, videos), jnp.int32),
            pltpu.VMEM((1, videos), jnp.int32),
            pltpu.VMEM((videos, length, places, channels), BF16),
            pltpu.VMEM((3 * channels, channels), BF16),
            pltpu.VMEM((3 * channels, channels), BF16),
            pltpu.VMEM((1, channels), F32),
            pltpu.VMEM((1, channels), F32),
            pltpu.VMEM((1, 128), jnp.int32),
            pltpu.SMEM((1, 128), jnp.int32),
            pltpu.VMEM((2, videos, places, channels), BF16),
            pltpu.VMEM((rows, channels), BF16),
            pltpu.VMEM((rows, channels), BF16),
            pltpu.VMEM((rows, channels), BF16),
            pltpu.VMEM((rows, channels), BF16),
            pltpu.VMEM((4, rows, channels), BF16),
            pltpu.VMEM((videos, 8, channels), F32),
            pltpu.VMEM((videos, 8, channels), F32),
            pltpu.VMEM((4,) + message, F32),
            pltpu.VMEM((4,) + message, F32),
            pltpu.VMEM(message, F32),
            pltpu.VMEM(message, F32),
            pltpu.VMEM((4, videos, 128), F32),
            pltpu.VMEM((4, videos, 128), F32),
            pltpu.VMEM((videos, channels), F32),
            pltpu.VMEM((videos, channels), F32),
            pltpu.VMEM((videos, places, channels), BF16),
            pltpu.VMEM((videos, places, channels), BF16),
            pltpu.VMEM((2, loads, 2, places, channels), BF16),
            pltpu.VMEM((loads, 2, places, channels), BF16),
            pltpu.VMEM((loads, 2, places, channels), BF16),
            pltpu.VMEM((8, 128), jnp.int32),
            pltpu.VMEM((loads, 8, 128), jnp.int32),
            pltpu.SMEM((videos // 2,), jnp.int32),
            pltpu.SemaphoreType.DMA((12,)),
            pltpu.SemaphoreType.DMA((4,)),
            pltpu.SemaphoreType.DMA((videos // min(8, videos),)),
            pltpu.SemaphoreType.DMA((videos // min(8, videos),)),
            pltpu.SemaphoreType.DMA((3,)),
            pltpu.SemaphoreType.DMA((3,)),
            pltpu.SemaphoreType.REGULAR,
            pltpu.SemaphoreType.DMA((2,)),
            pltpu.SemaphoreType.DMA((3,)),
            pltpu.SemaphoreType.DMA((3,)),
            pltpu.SemaphoreType.DMA((2,)),
            pltpu.SemaphoreType.DMA((2,)),
        ],
        compiler_params=pltpu.CompilerParams(
            collective_id=0, has_side_effects=True, vmem_limit_bytes=63 * 1024 * 1024
        ),
    )(
        counts,
        dest.reshape(1, videos),
        frames[0],
        first_weight.reshape(3 * channels, channels),
        second_weight.reshape(3 * channels, channels),
        gain.reshape(1, channels),
        bias.reshape(1, channels),
    )
    return result[None]


def solution(mesh):
    loads, spans = mesh.shape["load"], mesh.shape["tm"]
    return jax.shard_map(
        functools.partial(body, loads, spans),
        mesh=mesh,
        in_specs=(
            P("tm", "load", None, None, None),
            P("tm", "load"),
            P("load"),
            P(),
            P(),
            P(),
            P(),
        ),
        out_specs=P("tm", "load", None, None, None),
        check_vma=False,
    )
```

```python
import functools

import jax
import jax.numpy as jnp
from jax import lax
from jax.experimental import pallas as pl
from jax.experimental.pallas import tpu as pltpu
from jax.sharding import PartitionSpec as P

F32 = jnp.float32
BF16 = jnp.bfloat16
MESH = pl.DeviceIdType.MESH


def flat(x):
    videos, places, channels = x.shape
    return x.astype(F32).reshape(videos * places, channels).astype(BF16)


def dot(a, b):
    return jnp.dot(a, b, preferred_element_type=F32)


def silu(x):
    h = 0.5 * x
    return h + h * jnp.tanh(h)


def kernel(
    loads,
    spans,
    group,
    counts_hbm,
    dest_hbm,
    frames_hbm,
    w1_hbm,
    w2_hbm,
    gain_hbm,
    bias_hbm,
    out,
    cnt_s,
    cnt_v,
    dest_v,
    frames,
    w1,
    w2,
    gain,
    bias,
    pack_v,
    pack_s,
    tail,
    t1_send,
    t1_recv,
    t2_send,
    t2_recv,
    first,
    acc1,
    acc2,
    a_send,
    a_recv,
    b_send,
    b_recv,
    c_send,
    c_recv,
    mean_v,
    scale_v,
    enc_0,
    enc_1,
    stage,
    recv_0,
    recv_1,
    d_send,
    d_recv,
    table,
    sem_in,
    sem_t,
    sem_c_send,
    sem_c_recv,
    sem_a_send,
    sem_a_recv,
    sem_ready,
    sem_b,
    sem_s_send,
    sem_s_recv,
    sem_x_send,
    sem_x_recv,
):
    videos, places, channels = frames.shape[0], frames.shape[2], frames.shape[3]
    length = frames.shape[1]
    quarter = channels // 4
    rows = group * places
    pairs = videos // 2
    me = lax.axis_index("load")
    t = lax.axis_index("tm")
    team = t // 4
    seat = t % 4
    after = lax.rem(t + 1, spans)
    beyond = lax.rem(t + jnp.where(seat == 0, spans - 1, 1), spans)
    has_before, has_after = t > 0, t < spans - 1
    team_before, team_after = t >= 4, t < spans - 4
    edge = jnp.logical_or(jnp.logical_and(seat == 0, has_before), jnp.logical_and(seat == 3, has_after))

    pieces = 4
    part = videos // pieces
    fetches = [
        pltpu.make_async_copy(a, b, sem_in.at[i])
        for i, (a, b) in enumerate(
            [(counts_hbm, cnt_s), (counts_hbm, cnt_v), (dest_hbm, dest_v)]
            + [(frames_hbm.at[pl.ds(q * part, part)], frames.at[pl.ds(q * part, part)]) for q in range(pieces)]
            + [(w1_hbm, w1), (w2_hbm, w2), (gain_hbm, gain), (bias_hbm, bias)]
        )
    ]
    for fetch in fetches:
        fetch.start()

    enc = (enc_0, enc_1)
    recv = (recv_0, recv_1)
    barrier = pltpu.get_barrier_semaphore()

    def greet(load, place):
        pl.semaphore_signal(barrier, inc=1, device_id=(load, place), device_id_type=MESH)

    @pl.when(edge)
    def _():
        greet(me, beyond)

    for s in range(1, 4):
        greet(me, team * 4 + lax.rem(seat + s, 4))

    @pl.when(team_after)
    def _():
        greet(me, lax.rem(t + 4, spans))

    @pl.loop(1, loads)
    def _(s):
        greet(lax.rem(me + s, loads), t)

    for fetch in fetches[:-3]:
        fetch.wait()

    @pl.loop(0, videos)
    def _(v):
        tail[0, v] = frames[v, jnp.clip(cnt_s[0, v] - 2, 0, length - 1)]
        tail[1, v] = frames[v, jnp.clip(cnt_s[0, v] - 1, 0, length - 1)]

    @pl.loop(0, videos // group)
    def _(g):
        at = pl.ds(g * group, group)
        lhs = jnp.concatenate([flat(tail[0, at]), flat(tail[1, at])], axis=1)
        t1_send[pl.ds(pl.multiple_of(g * rows, rows), rows)] = dot(lhs, w1[: 2 * channels]).astype(BF16)

    lanes = 128
    row = jnp.pad(dest_v[...], ((0, 7), (0, lanes - videos)), constant_values=-1)
    d_send[...] = row

    pl.semaphore_wait(barrier, 3 + (loads - 1) + jnp.where(edge, 1, 0) + jnp.where(team_before, 1, 0))

    @pl.when(team_before)
    def _():
        pl.semaphore_signal(
            sem_ready, inc=1, device_id=(me, lax.rem(t + spans - 4, spans)), device_id_type=MESH
        )

    def remote(src, dst, ss, rs, load, place):
        return pltpu.make_async_remote_copy(
            src_ref=src, dst_ref=dst, send_sem=ss, recv_sem=rs, device_id=(load, place), device_id_type=MESH
        )

    def context(g):
        place = pl.ds(pl.multiple_of(g * rows, rows), rows)
        return remote(t1_send.at[place], t1_recv.at[place], sem_c_send.at[g], sem_c_recv.at[g], me, after)

    @pl.when(has_after)
    def _():
        for g in range(videos // group):
            context(g).start()

    d_recv[me] = row

    def column(values):
        r = lax.broadcasted_iota(jnp.int32, (videos, videos), 0)
        c = lax.broadcasted_iota(jnp.int32, (videos, videos), 1)
        return jnp.sum(jnp.where(r == c, values, 0), axis=1, keepdims=True)

    for fetch in fetches[-3:]:
        fetch.wait()
    counts_row = cnt_v[...]

    def add_sums(g, at, values, fresh):
        tiles = values.reshape(group, places // 8, 8, channels)
        s1 = jnp.sum(tiles, axis=1)
        s2 = jnp.sum(tiles * tiles, axis=1)
        if fresh:
            acc1[at] = s1
            acc2[at] = s2
        else:
            acc1[at] += s1
            acc2[at] += s2

    def group_live(g, step, limit_of):
        parts = [limit_of(cnt_s[0, g * group + i]) > step for i in range(group)]
        return parts

    def masked(value, flags):
        pieces = value.reshape(group, places, channels)
        return jnp.concatenate(
            [jnp.where(flags[i], pieces[i : i + 1], 0.0) for i in range(group)], axis=0
        )

    @pl.loop(0, videos // group)
    def _(g):
        at = pl.ds(g * group, group)
        place = pl.ds(pl.multiple_of(g * rows, rows), rows)
        for j in range(1, 4):
            lhs = jnp.concatenate([flat(frames[at, 2 * j - 2 + k]) for k in range(3)], axis=1)
            value = masked(silu(dot(lhs, w1[...])), group_live(g, 2 * j, lambda n: n))
            value = value.reshape(rows, channels).astype(BF16)
            first[j, place] = value
            add_sums(g, at, value.astype(F32), j == 1)

    @pl.loop(1, loads)
    def _(s):
        remote(d_send, d_recv.at[me], sem_t.at[2], sem_t.at[3], lax.rem(me + s, loads), t).start()

    @pl.loop(0, videos // group)
    def _(g):
        at = pl.ds(g * group, group)
        place = pl.ds(pl.multiple_of(g * rows, rows), rows)

        @pl.when(has_before)
        def _():
            context(g).wait_recv()

        part = jnp.where(has_before, t1_recv[place].astype(F32), 0.0)
        value = silu(part + dot(flat(frames[at, 0]), w1[2 * channels :])).astype(BF16)
        first[0, place] = value
        add_sums(g, at, value.astype(F32), False)

    s1 = jnp.sum(acc1[...], axis=1)
    s2 = jnp.sum(acc2[...], axis=1)
    num = (((counts_row + 1) // 2) * places).astype(F32)
    num = jnp.pad(num, ((0, 7), (0, lanes - videos)))

    def parts(x):
        return [x[:, r * quarter : (r + 1) * quarter] for r in range(4)]

    for r, (p1, p2) in enumerate(zip(parts(s1), parts(s2))):
        a_send[r] = jnp.concatenate([jnp.concatenate([p1, p2], axis=1), num], axis=0)

    def mates(source, target, ss, rs):
        made = []
        for s in range(1, 4):
            mate = lax.rem(seat + s, 4)
            made.append(
                remote(source.at[mate], target.at[seat], ss.at[s - 1], rs.at[s - 1], me, team * 4 + mate)
            )
        return made

    a_copies = mates(a_send, a_recv, sem_a_send, sem_a_recv)
    for copy in a_copies:
        copy.start()
    a_recv[seat] = a_send[seat]

    place_of = column(dest_v[...])
    place_of = place_of // videos * 2 + place_of % 2
    lane = lax.broadcasted_iota(jnp.int32, (videos, 128), 1)
    video = lax.broadcasted_iota(jnp.int32, (videos, 128), 0)
    pack_v[...] = jnp.clip(jnp.sum(jnp.where(place_of == lane, video, 0), axis=0, keepdims=True), 0, videos - 1)
    to_scalars = pltpu.make_async_copy(pack_v, pack_s, sem_in.at[len(fetches)])
    to_scalars.start()

    my_gain = sum(jnp.where(seat == r, g, 0.0) for r, g in enumerate(parts(gain[...])))
    my_gain = jnp.concatenate([my_gain, my_gain], axis=1)
    for s in range(1, 4):
        from_mate = lax.rem(seat + 4 - s, 4)
        remote(
            a_send.at[0], a_recv.at[from_mate], sem_a_send.at[s - 1], sem_a_recv.at[s - 1], me, after
        ).wait_recv()
    totals = [a_recv[0]]
    for r in range(1, 4):
        totals.append(totals[-1] + a_recv[r])
    b_copy = remote(b_send, b_recv, sem_b.at[0], sem_b.at[1], me, lax.rem(t + 4, spans))

    @pl.when(team_before)
    def _():
        b_copy.wait_recv()

    base = jnp.where(team_before, b_recv[...], 0.0)
    b_send[...] = base + totals[-1]

    @pl.when(team_after)
    def _():
        pl.semaphore_wait(sem_ready, 1)
        b_copy.start()

    in_low = lax.broadcasted_iota(jnp.int32, (videos, lanes), 1) < quarter
    for r in range(4):
        total = base + totals[r]
        value = total[:videos] / column(total[videos : videos + 1, :videos])
        swapped = jnp.concatenate([value[:, quarter:], value[:, :quarter]], axis=1)
        var = value - swapped * swapped
        c_send[r] = jnp.where(in_low, value, lax.rsqrt(var + 1e-05) * my_gain)
    c_copies = mates(c_send, c_recv, sem_s_send, sem_s_recv)
    for copy in c_copies:
        copy.start()
    c_recv[seat] = c_send[seat]
    for s in range(1, 4):
        from_mate = lax.rem(seat + 4 - s, 4)
        remote(
            c_send.at[0], c_recv.at[from_mate], sem_s_send.at[s - 1], sem_s_recv.at[s - 1], me, after
        ).wait_recv()
    mean_v[...] = jnp.concatenate([c_recv[r][:, :quarter] for r in range(4)], axis=1)
    scale_v[...] = jnp.concatenate([c_recv[r][:, quarter:] for r in range(4)], axis=1)

    def exchange(i):
        stage[i, me, 0] = enc[i][pack_s[0, 2 * me]]
        stage[i, me, 1] = enc[i][pack_s[0, 2 * me + 1]]
        recv[i][me] = stage[i, me]

        @pl.loop(1, loads)
        def _(s):
            to = lax.rem(me + s, loads)
            stage[i, to, 0] = enc[i][pack_s[0, 2 * to]]
            stage[i, to, 1] = enc[i][pack_s[0, 2 * to + 1]]
            remote(stage.at[i, to], recv[i].at[me], sem_x_send.at[i], sem_x_recv.at[i], to, t).start()

    def all_of(i):
        sent = pl.ds(0, loads - 1)
        return remote(stage.at[i, sent], recv[i].at[sent], sem_x_send.at[i], sem_x_recv.at[i], me, after)

    @pl.loop(0, videos // group)
    def _(g):
        at = pl.ds(pl.multiple_of(g * group, group), group)
        place = pl.ds(pl.multiple_of(g * rows, rows), rows)
        mean = mean_v[at][:, None, :]
        scale = scale_v[at][:, None, :]
        taps = []
        for j in range(3):
            value = first[j, place].astype(F32).reshape(group, places, channels)
            value = ((value - mean) * scale).reshape(rows, channels).astype(BF16)
            first[j, place] = value
            taps.append(value)
        lhs = jnp.concatenate(taps, axis=1)
        value = masked(dot(lhs, w2[...]) + bias[...], group_live(g, 2, lambda n: (n + 1) // 2))
        enc_1[at] = value.astype(BF16)

    to_scalars.wait()
    exchange(1)

    @pl.loop(0, videos // group)
    def _(g):
        place = pl.ds(pl.multiple_of(g * rows, rows), rows)
        at = pl.ds(pl.multiple_of(g * group, group), group)
        normed = [first[j, place].astype(F32).reshape(group, places, channels) for j in range(4)]
        normed[3] = (normed[3] - mean_v[at][:, None, :]) * scale_v[at][:, None, :]
        ends = []
        for k in range(2):
            pieces = []
            for i in range(group):
                n = (cnt_s[0, g * group + i] + 1) // 2
                pieces.append(
                    jnp.where(
                        n == 2,
                        normed[k][i : i + 1],
                        jnp.where(n == 3, normed[k + 1][i : i + 1], normed[k + 2][i : i + 1]),
                    )
                )
            ends.append(jnp.concatenate(pieces, axis=0).reshape(rows, channels).astype(BF16))
        t2_send[place] = dot(jnp.concatenate(ends, axis=1), w2[: 2 * channels]).astype(BF16)

    t2 = remote(t2_send, t2_recv, sem_t.at[0], sem_t.at[1], me, after)

    @pl.when(has_after)
    def _():
        t2.start()


    @pl.when(has_before)
    def _():
        t2.wait_recv()

    @pl.loop(0, videos // group)
    def _(g):
        at = pl.ds(g * group, group)
        place = pl.ds(pl.multiple_of(g * rows, rows), rows)
        part = jnp.where(has_before, t2_recv[place].astype(F32), 0.0)
        value = part + dot(first[0, place], w2[2 * channels :]) + bias[...]
        enc_0[at] = value.reshape(group, places, channels).astype(BF16)

    exchange(0)

    others = pl.ds(0, loads - 1)
    remote(d_recv.at[others], d_recv.at[others], sem_t.at[2], sem_t.at[3], me, after).wait()
    known = d_recv[...][:, 0, :]
    loader = lax.broadcasted_iota(jnp.int32, known.shape, 0)
    for i in range(pairs):
        table[i] = jnp.clip(jnp.sum(jnp.where(known == me * videos + 2 * i, loader, 0)), 0, loads - 1)

    for copy in a_copies + c_copies:
        copy.wait_send()

    @pl.when(has_after)
    def _():
        for g in range(videos // group):
            context(g).wait_send()
        t2.wait_send()

    @pl.when(team_after)
    def _():
        b_copy.wait_send()


    for i in (1, 0):
        all_of(i).wait_recv()

        @pl.loop(0, pairs)
        def _(q):
            out[2 * q, i] = recv[i][table[q], 0]
            out[2 * q + 1, i] = recv[i][table[q], 1]

        all_of(i).wait_send()


def body(loads, spans, frames, counts, dest, first_weight, second_weight, gain, bias):
    videos, length, places, channels = frames.shape[1:]
    group = min(16, videos)
    rows = videos * places
    vmem = pl.BlockSpec(memory_space=pltpu.VMEM)
    hbm = pl.BlockSpec(memory_space=pltpu.HBM)
    message = (videos + 8, 128)
    result = pl.pallas_call(
        functools.partial(kernel, loads, spans, group),
        out_shape=jax.ShapeDtypeStruct((videos, 2, places, channels), BF16),
        in_specs=[hbm] * 7,
        out_specs=vmem,
        scratch_shapes=[
            pltpu.SMEM((1, videos), jnp.int32),
            pltpu.VMEM((1, videos), jnp.int32),
            pltpu.VMEM((1, videos), jnp.int32),
            pltpu.VMEM((videos, length, places, channels), BF16),
            pltpu.VMEM((3 * channels, channels), BF16),
            pltpu.VMEM((3 * channels, channels), BF16),
            pltpu.VMEM((1, channels), F32),
            pltpu.VMEM((1, channels), F32),
            pltpu.VMEM((1, 128), jnp.int32),
            pltpu.SMEM((1, 128), jnp.int32),
            pltpu.VMEM((2, videos, places, channels), BF16),
            pltpu.VMEM((rows, channels), BF16),
            pltpu.VMEM((rows, channels), BF16),
            pltpu.VMEM((rows, channels), BF16),
            pltpu.VMEM((rows, channels), BF16),
            pltpu.VMEM((4, rows, channels), BF16),
            pltpu.VMEM((videos, 8, channels), F32),
            pltpu.VMEM((videos, 8, channels), F32),
            pltpu.VMEM((4,) + message, F32),
            pltpu.VMEM((4,) + message, F32),
            pltpu.VMEM(message, F32),
            pltpu.VMEM(message, F32),
            pltpu.VMEM((4, videos, 128), F32),
            pltpu.VMEM((4, videos, 128), F32),
            pltpu.VMEM((videos, channels), F32),
            pltpu.VMEM((videos, channels), F32),
            pltpu.VMEM((videos, places, channels), BF16),
            pltpu.VMEM((videos, places, channels), BF16),
            pltpu.VMEM((2, loads, 2, places, channels), BF16),
            pltpu.VMEM((loads, 2, places, channels), BF16),
            pltpu.VMEM((loads, 2, places, channels), BF16),
            pltpu.VMEM((8, 128), jnp.int32),
            pltpu.VMEM((loads, 8, 128), jnp.int32),
            pltpu.SMEM((videos // 2,), jnp.int32),
            pltpu.SemaphoreType.DMA((12,)),
            pltpu.SemaphoreType.DMA((4,)),
            pltpu.SemaphoreType.DMA((videos // group,)),
            pltpu.SemaphoreType.DMA((videos // group,)),
            pltpu.SemaphoreType.DMA((3,)),
            pltpu.SemaphoreType.DMA((3,)),
            pltpu.SemaphoreType.REGULAR,
            pltpu.SemaphoreType.DMA((2,)),
            pltpu.SemaphoreType.DMA((3,)),
            pltpu.SemaphoreType.DMA((3,)),
            pltpu.SemaphoreType.DMA((2,)),
            pltpu.SemaphoreType.DMA((2,)),
        ],
        compiler_params=pltpu.CompilerParams(
            collective_id=0, has_side_effects=True, vmem_limit_bytes=48 * 1024 * 1024
        ),
    )(
        *(
            pltpu.with_memory_space_constraint(operand, pltpu.HBM)
            for operand in (
                counts,
                dest.reshape(1, videos),
                frames[0],
                first_weight.reshape(3 * channels, channels),
                second_weight.reshape(3 * channels, channels),
                gain.reshape(1, channels),
                bias.reshape(1, channels),
            )
        )
    )
    return result[None]


def solution(mesh):
    loads, spans = mesh.shape["load"], mesh.shape["tm"]
    return jax.shard_map(
        functools.partial(body, loads, spans),
        mesh=mesh,
        in_specs=(
            P("tm", "load", None, None, None),
            P("tm", "load"),
            P("load"),
            P(),
            P(),
            P(),
            P(),
        ),
        out_specs=P("tm", "load", None, None, None),
        check_vma=False,
    )
```

```python
import functools

import jax
import jax.numpy as jnp
from jax import lax
from jax.experimental import pallas as pl
from jax.experimental.pallas import tpu as pltpu
from jax.sharding import PartitionSpec as P

F32 = jnp.float32
BF16 = jnp.bfloat16
MESH = pl.DeviceIdType.MESH


def flat(x):
    videos, places, channels = x.shape
    return x.astype(F32).reshape(videos * places, channels).astype(BF16)


def dot(a, b):
    return jnp.dot(a, b, preferred_element_type=F32)


def silu(x):
    h = 0.5 * x
    return h + h * jnp.tanh(h)


def kernel(
    loads,
    spans,
    group,
    counts_hbm,
    dest_hbm,
    frames_hbm,
    w1_hbm,
    w2_hbm,
    gain_hbm,
    bias_hbm,
    out,
    cnt_s,
    cnt_v,
    dest_v,
    frames,
    w1,
    w2,
    gain,
    bias,
    pack_v,
    pack_s,
    tail,
    t1_send,
    t1_recv,
    t2_send,
    t2_recv,
    first,
    acc1,
    acc2,
    a_send,
    a_recv,
    b_send,
    b_recv,
    c_send,
    c_recv,
    mean_v,
    scale_v,
    enc_0,
    enc_1,
    stage,
    recv_0,
    recv_1,
    d_send,
    d_recv,
    table,
    sem_in,
    sem_t,
    sem_c_send,
    sem_c_recv,
    sem_a_send,
    sem_a_recv,
    sem_ready,
    sem_b,
    sem_s_send,
    sem_s_recv,
    sem_x_send,
    sem_x_recv,
):
    videos, places, channels = frames.shape[0], frames.shape[2], frames.shape[3]
    length = frames.shape[1]
    quarter = channels // 4
    rows = group * places
    pairs = videos // 2
    me = lax.axis_index("load")
    t = lax.axis_index("tm")
    team = t // 4
    seat = t % 4
    after = lax.rem(t + 1, spans)
    beyond = lax.rem(t + jnp.where(seat == 0, spans - 1, 1), spans)
    has_before, has_after = t > 0, t < spans - 1
    teams = spans // 4
    edge = jnp.logical_or(jnp.logical_and(seat == 0, has_before), jnp.logical_and(seat == 3, has_after))

    pieces = 4
    part = videos // pieces
    fetches = [
        pltpu.make_async_copy(a, b, sem_in.at[i])
        for i, (a, b) in enumerate(
            [(counts_hbm, cnt_s), (counts_hbm, cnt_v), (dest_hbm, dest_v)]
            + [(frames_hbm.at[pl.ds(q * part, part)], frames.at[pl.ds(q * part, part)]) for q in range(pieces)]
            + [(w1_hbm, w1), (w2_hbm, w2), (gain_hbm, gain), (bias_hbm, bias)]
        )
    ]
    for fetch in fetches:
        fetch.start()

    enc = (enc_0, enc_1)
    recv = (recv_0, recv_1)
    barrier = pltpu.get_barrier_semaphore()

    def greet(load, place):
        pl.semaphore_signal(barrier, inc=1, device_id=(load, place), device_id_type=MESH)

    @pl.when(edge)
    def _():
        greet(me, beyond)

    for s in range(1, 4):
        greet(me, team * 4 + lax.rem(seat + s, 4))

    for s in range(1, teams):

        @pl.when(team + s < teams)
        def _():
            greet(me, lax.rem(t + 4 * s, spans))

    @pl.loop(1, loads)
    def _(s):
        greet(lax.rem(me + s, loads), t)

    for fetch in fetches[:-3]:
        fetch.wait()

    @pl.loop(0, videos)
    def _(v):
        tail[0, v] = frames[v, jnp.clip(cnt_s[0, v] - 2, 0, length - 1)]
        tail[1, v] = frames[v, jnp.clip(cnt_s[0, v] - 1, 0, length - 1)]

    @pl.loop(0, videos // group)
    def _(g):
        at = pl.ds(g * group, group)
        lhs = jnp.concatenate([flat(tail[0, at]), flat(tail[1, at])], axis=1)
        t1_send[pl.ds(pl.multiple_of(g * rows, rows), rows)] = dot(lhs, w1[: 2 * channels]).astype(BF16)

    lanes = 128
    row = jnp.pad(dest_v[...], ((0, 7), (0, lanes - videos)), constant_values=-1)
    d_send[...] = row

    pl.semaphore_wait(barrier, 3 + (loads - 1) + jnp.where(edge, 1, 0) + team)

    for s in range(1, teams):

        @pl.when(team >= s)
        def _():
            pl.semaphore_signal(
                sem_ready.at[s - 1],
                inc=1,
                device_id=(me, lax.rem(t + spans - 4 * s, spans)),
                device_id_type=MESH,
            )

    def remote(src, dst, ss, rs, load, place):
        return pltpu.make_async_remote_copy(
            src_ref=src, dst_ref=dst, send_sem=ss, recv_sem=rs, device_id=(load, place), device_id_type=MESH
        )

    def context(g):
        place = pl.ds(pl.multiple_of(g * rows, rows), rows)
        return remote(t1_send.at[place], t1_recv.at[place], sem_c_send.at[g], sem_c_recv.at[g], me, after)

    @pl.when(has_after)
    def _():
        for g in range(videos // group):
            context(g).start()

    d_recv[me] = row

    def column(values):
        r = lax.broadcasted_iota(jnp.int32, (videos, videos), 0)
        c = lax.broadcasted_iota(jnp.int32, (videos, videos), 1)
        return jnp.sum(jnp.where(r == c, values, 0), axis=1, keepdims=True)

    for fetch in fetches[-3:]:
        fetch.wait()
    counts_row = cnt_v[...]

    def add_sums(g, at, values, fresh):
        tiles = values.reshape(group, places // 8, 8, channels)
        s1 = jnp.sum(tiles, axis=1)
        s2 = jnp.sum(tiles * tiles, axis=1)
        if fresh:
            acc1[at] = s1
            acc2[at] = s2
        else:
            acc1[at] += s1
            acc2[at] += s2

    def group_live(g, step, limit_of):
        parts = [limit_of(cnt_s[0, g * group + i]) > step for i in range(group)]
        return parts

    def masked(value, flags):
        pieces = value.reshape(group, places, channels)
        return jnp.concatenate(
            [jnp.where(flags[i], pieces[i : i + 1], 0.0) for i in range(group)], axis=0
        )

    @pl.loop(0, videos // group)
    def _(g):
        at = pl.ds(g * group, group)
        place = pl.ds(pl.multiple_of(g * rows, rows), rows)
        for j in range(1, 4):
            lhs = jnp.concatenate([flat(frames[at, 2 * j - 2 + k]) for k in range(3)], axis=1)
            value = masked(silu(dot(lhs, w1[...])), group_live(g, 2 * j, lambda n: n))
            value = value.reshape(rows, channels).astype(BF16)
            first[j, place] = value
            add_sums(g, at, value.astype(F32), j == 1)

    @pl.loop(1, loads)
    def _(s):
        remote(d_send, d_recv.at[me], sem_t.at[2], sem_t.at[3], lax.rem(me + s, loads), t).start()

    @pl.loop(0, videos // group)
    def _(g):
        at = pl.ds(g * group, group)
        place = pl.ds(pl.multiple_of(g * rows, rows), rows)

        @pl.when(has_before)
        def _():
            context(g).wait_recv()

        part = jnp.where(has_before, t1_recv[place].astype(F32), 0.0)
        value = silu(part + dot(flat(frames[at, 0]), w1[2 * channels :])).astype(BF16)
        first[0, place] = value
        add_sums(g, at, value.astype(F32), False)

    s1 = jnp.sum(acc1[...], axis=1)
    s2 = jnp.sum(acc2[...], axis=1)
    num = (((counts_row + 1) // 2) * places).astype(F32)
    num = jnp.pad(num, ((0, 7), (0, lanes - videos)))

    def parts(x):
        return [x[:, r * quarter : (r + 1) * quarter] for r in range(4)]

    for r, (p1, p2) in enumerate(zip(parts(s1), parts(s2))):
        a_send[r] = jnp.concatenate([jnp.concatenate([p1, p2], axis=1), num], axis=0)

    def mates(source, target, ss, rs):
        made = []
        for s in range(1, 4):
            mate = lax.rem(seat + s, 4)
            made.append(
                remote(source.at[mate], target.at[seat], ss.at[s - 1], rs.at[s - 1], me, team * 4 + mate)
            )
        return made

    a_copies = mates(a_send, a_recv, sem_a_send, sem_a_recv)
    for copy in a_copies:
        copy.start()
    a_recv[seat] = a_send[seat]

    place_of = column(dest_v[...])
    place_of = place_of // videos * 2 + place_of % 2
    lane = lax.broadcasted_iota(jnp.int32, (videos, 128), 1)
    video = lax.broadcasted_iota(jnp.int32, (videos, 128), 0)
    pack_v[...] = jnp.clip(jnp.sum(jnp.where(place_of == lane, video, 0), axis=0, keepdims=True), 0, videos - 1)
    to_scalars = pltpu.make_async_copy(pack_v, pack_s, sem_in.at[len(fetches)])
    to_scalars.start()

    my_gain = sum(jnp.where(seat == r, g, 0.0) for r, g in enumerate(parts(gain[...])))
    my_gain = jnp.concatenate([my_gain, my_gain], axis=1)
    for s in range(1, 4):
        from_mate = lax.rem(seat + 4 - s, 4)
        remote(
            a_send.at[0], a_recv.at[from_mate], sem_a_send.at[s - 1], sem_a_recv.at[s - 1], me, after
        ).wait_recv()
    totals = [a_recv[0]]
    for r in range(1, 4):
        totals.append(totals[-1] + a_recv[r])
    def totals_to(s):
        return remote(
            b_send, b_recv.at[s - 1], sem_b.at[0, s - 1], sem_b.at[1, s - 1], me, lax.rem(t + 4 * s, spans)
        )

    b_send[...] = totals[-1]
    for s in range(1, teams):

        @pl.when(team + s < teams)
        def _():
            pl.semaphore_wait(sem_ready.at[s - 1], 1)
            totals_to(s).start()

    base = jnp.zeros_like(totals[0])
    for s in range(teams - 1, 0, -1):

        @pl.when(team >= s)
        def _():
            totals_to(s).wait_recv()

        base = base + jnp.where(team >= s, b_recv[s - 1], 0.0)

    in_low = lax.broadcasted_iota(jnp.int32, (videos, lanes), 1) < quarter
    for r in range(4):
        total = base + totals[r]
        value = total[:videos] / column(total[videos : videos + 1, :videos])
        swapped = jnp.concatenate([value[:, quarter:], value[:, :quarter]], axis=1)
        var = value - swapped * swapped
        c_send[r] = jnp.where(in_low, value, lax.rsqrt(var + 1e-05) * my_gain)
    c_copies = mates(c_send, c_recv, sem_s_send, sem_s_recv)
    for copy in c_copies:
        copy.start()
    c_recv[seat] = c_send[seat]
    for s in range(1, 4):
        from_mate = lax.rem(seat + 4 - s, 4)
        remote(
            c_send.at[0], c_recv.at[from_mate], sem_s_send.at[s - 1], sem_s_recv.at[s - 1], me, after
        ).wait_recv()
    mean_v[...] = jnp.concatenate([c_recv[r][:, :quarter] for r in range(4)], axis=1)
    scale_v[...] = jnp.concatenate([c_recv[r][:, quarter:] for r in range(4)], axis=1)

    def exchange(i):
        stage[i, me, 0] = enc[i][pack_s[0, 2 * me]]
        stage[i, me, 1] = enc[i][pack_s[0, 2 * me + 1]]
        recv[i][me] = stage[i, me]

        @pl.loop(1, loads)
        def _(s):
            to = lax.rem(me + s, loads)
            stage[i, to, 0] = enc[i][pack_s[0, 2 * to]]
            stage[i, to, 1] = enc[i][pack_s[0, 2 * to + 1]]
            remote(stage.at[i, to], recv[i].at[me], sem_x_send.at[i], sem_x_recv.at[i], to, t).start()

    def all_of(i):
        sent = pl.ds(0, loads - 1)
        return remote(stage.at[i, sent], recv[i].at[sent], sem_x_send.at[i], sem_x_recv.at[i], me, after)

    @pl.loop(0, videos // group)
    def _(g):
        at = pl.ds(pl.multiple_of(g * group, group), group)
        place = pl.ds(pl.multiple_of(g * rows, rows), rows)
        mean = mean_v[at][:, None, :]
        scale = scale_v[at][:, None, :]
        taps = []
        for j in range(3):
            value = first[j, place].astype(F32).reshape(group, places, channels)
            value = ((value - mean) * scale).reshape(rows, channels).astype(BF16)
            first[j, place] = value
            taps.append(value)
        lhs = jnp.concatenate(taps, axis=1)
        value = masked(dot(lhs, w2[...]) + bias[...], group_live(g, 2, lambda n: (n + 1) // 2))
        enc_1[at] = value.astype(BF16)

    to_scalars.wait()
    exchange(1)

    @pl.loop(0, videos // group)
    def _(g):
        place = pl.ds(pl.multiple_of(g * rows, rows), rows)
        at = pl.ds(pl.multiple_of(g * group, group), group)
        normed = [first[j, place].astype(F32).reshape(group, places, channels) for j in range(4)]
        normed[3] = (normed[3] - mean_v[at][:, None, :]) * scale_v[at][:, None, :]
        ends = []
        for k in range(2):
            pieces = []
            for i in range(group):
                n = (cnt_s[0, g * group + i] + 1) // 2
                pieces.append(
                    jnp.where(
                        n == 2,
                        normed[k][i : i + 1],
                        jnp.where(n == 3, normed[k + 1][i : i + 1], normed[k + 2][i : i + 1]),
                    )
                )
            ends.append(jnp.concatenate(pieces, axis=0).reshape(rows, channels).astype(BF16))
        t2_send[place] = dot(jnp.concatenate(ends, axis=1), w2[: 2 * channels]).astype(BF16)

    t2 = remote(t2_send, t2_recv, sem_t.at[0], sem_t.at[1], me, after)

    @pl.when(has_after)
    def _():
        t2.start()


    @pl.when(has_before)
    def _():
        t2.wait_recv()

    @pl.loop(0, videos // group)
    def _(g):
        at = pl.ds(g * group, group)
        place = pl.ds(pl.multiple_of(g * rows, rows), rows)
        part = jnp.where(has_before, t2_recv[place].astype(F32), 0.0)
        value = part + dot(first[0, place], w2[2 * channels :]) + bias[...]
        enc_0[at] = value.reshape(group, places, channels).astype(BF16)

    exchange(0)

    others = pl.ds(0, loads - 1)
    remote(d_recv.at[others], d_recv.at[others], sem_t.at[2], sem_t.at[3], me, after).wait()
    known = d_recv[...][:, 0, :]
    loader = lax.broadcasted_iota(jnp.int32, known.shape, 0)
    for i in range(pairs):
        table[i] = jnp.clip(jnp.sum(jnp.where(known == me * videos + 2 * i, loader, 0)), 0, loads - 1)

    for copy in a_copies + c_copies:
        copy.wait_send()

    @pl.when(has_after)
    def _():
        for g in range(videos // group):
            context(g).wait_send()
        t2.wait_send()

    for s in range(1, teams):

        @pl.when(team + s < teams)
        def _():
            totals_to(s).wait_send()


    for i in (1, 0):
        all_of(i).wait_recv()

        @pl.loop(0, pairs)
        def _(q):
            out[2 * q, i] = recv[i][table[q], 0]
            out[2 * q + 1, i] = recv[i][table[q], 1]

        all_of(i).wait_send()


def body(loads, spans, frames, counts, dest, first_weight, second_weight, gain, bias):
    videos, length, places, channels = frames.shape[1:]
    group = min(16, videos)
    rows = videos * places
    vmem = pl.BlockSpec(memory_space=pltpu.VMEM)
    hbm = pl.BlockSpec(memory_space=pltpu.HBM)
    message = (videos + 8, 128)
    result = pl.pallas_call(
        functools.partial(kernel, loads, spans, group),
        out_shape=jax.ShapeDtypeStruct((videos, 2, places, channels), BF16),
        in_specs=[hbm] * 7,
        out_specs=vmem,
        scratch_shapes=[
            pltpu.SMEM((1, videos), jnp.int32),
            pltpu.VMEM((1, videos), jnp.int32),
            pltpu.VMEM((1, videos), jnp.int32),
            pltpu.VMEM((videos, length, places, channels), BF16),
            pltpu.VMEM((3 * channels, channels), BF16),
            pltpu.VMEM((3 * channels, channels), BF16),
            pltpu.VMEM((1, channels), F32),
            pltpu.VMEM((1, channels), F32),
            pltpu.VMEM((1, 128), jnp.int32),
            pltpu.SMEM((1, 128), jnp.int32),
            pltpu.VMEM((2, videos, places, channels), BF16),
            pltpu.VMEM((rows, channels), BF16),
            pltpu.VMEM((rows, channels), BF16),
            pltpu.VMEM((rows, channels), BF16),
            pltpu.VMEM((rows, channels), BF16),
            pltpu.VMEM((4, rows, channels), BF16),
            pltpu.VMEM((videos, 8, channels), F32),
            pltpu.VMEM((videos, 8, channels), F32),
            pltpu.VMEM((4,) + message, F32),
            pltpu.VMEM((4,) + message, F32),
            pltpu.VMEM(message, F32),
            pltpu.VMEM((spans // 4 - 1,) + message, F32),
            pltpu.VMEM((4, videos, 128), F32),
            pltpu.VMEM((4, videos, 128), F32),
            pltpu.VMEM((videos, channels), F32),
            pltpu.VMEM((videos, channels), F32),
            pltpu.VMEM((videos, places, channels), BF16),
            pltpu.VMEM((videos, places, channels), BF16),
            pltpu.VMEM((2, loads, 2, places, channels), BF16),
            pltpu.VMEM((loads, 2, places, channels), BF16),
            pltpu.VMEM((loads, 2, places, channels), BF16),
            pltpu.VMEM((8, 128), jnp.int32),
            pltpu.VMEM((loads, 8, 128), jnp.int32),
            pltpu.SMEM((videos // 2,), jnp.int32),
            pltpu.SemaphoreType.DMA((12,)),
            pltpu.SemaphoreType.DMA((4,)),
            pltpu.SemaphoreType.DMA((videos // group,)),
            pltpu.SemaphoreType.DMA((videos // group,)),
            pltpu.SemaphoreType.DMA((3,)),
            pltpu.SemaphoreType.DMA((3,)),
            pltpu.SemaphoreType.REGULAR((spans // 4 - 1,)),
            pltpu.SemaphoreType.DMA((2, spans // 4 - 1)),
            pltpu.SemaphoreType.DMA((3,)),
            pltpu.SemaphoreType.DMA((3,)),
            pltpu.SemaphoreType.DMA((2,)),
            pltpu.SemaphoreType.DMA((2,)),
        ],
        compiler_params=pltpu.CompilerParams(
            collective_id=0, has_side_effects=True, vmem_limit_bytes=48 * 1024 * 1024
        ),
    )(
        *(
            pltpu.with_memory_space_constraint(operand, pltpu.HBM)
            for operand in (
                counts,
                dest.reshape(1, videos),
                frames[0],
                first_weight.reshape(3 * channels, channels),
                second_weight.reshape(3 * channels, channels),
                gain.reshape(1, channels),
                bias.reshape(1, channels),
            )
        )
    )
    return result[None]


def solution(mesh):
    loads, spans = mesh.shape["load"], mesh.shape["tm"]
    return jax.shard_map(
        functools.partial(body, loads, spans),
        mesh=mesh,
        in_specs=(
            P("tm", "load", None, None, None),
            P("tm", "load"),
            P("load"),
            P(),
            P(),
            P(),
            P(),
        ),
        out_specs=P("tm", "load", None, None, None),
        check_vma=False,
    )
```

```python
import functools

import jax
import jax.numpy as jnp
from jax import lax
from jax.experimental import pallas as pl
from jax.experimental.pallas import tpu as pltpu
from jax.sharding import PartitionSpec as P

F32 = jnp.float32
BF16 = jnp.bfloat16
MESH = pl.DeviceIdType.MESH


def flat(x):
    videos, places, channels = x.shape
    return x.astype(F32).reshape(videos * places, channels).astype(BF16)


def dot(a, b):
    return jnp.dot(a, b, preferred_element_type=F32)


def silu(x):
    h = 0.5 * x
    return h + h * jnp.tanh(h)


def kernel(
    loads,
    spans,
    group,
    counts_hbm,
    dest_hbm,
    frames_hbm,
    w1_hbm,
    w2_hbm,
    gain_hbm,
    bias_hbm,
    out,
    cnt_s,
    cnt_v,
    dest_v,
    frames,
    w1,
    w2,
    gain,
    bias,
    pack_v,
    pack_s,
    tail,
    t1_send,
    t1_recv,
    t2_send,
    t2_recv,
    first,
    acc1,
    acc2,
    a_send,
    a_recv,
    b_send,
    b_recv,
    c_send,
    c_recv,
    mean_v,
    scale_v,
    enc_0,
    enc_1,
    stage,
    recv_0,
    recv_1,
    d_send,
    d_recv,
    table,
    sem_in,
    sem_t,
    sem_c_send,
    sem_c_recv,
    sem_a_send,
    sem_a_recv,
    sem_ready,
    sem_b,
    sem_s_send,
    sem_s_recv,
    sem_x_send,
    sem_x_recv,
):
    videos, places, channels = frames.shape[0], frames.shape[2], frames.shape[3]
    length = frames.shape[1]
    quarter = channels // 4
    rows = group * places
    pairs = videos // 2
    me = lax.axis_index("load")
    t = lax.axis_index("tm")
    team = t // 4
    seat = t % 4
    after = lax.rem(t + 1, spans)
    beyond = lax.rem(t + jnp.where(seat == 0, spans - 1, 1), spans)
    has_before, has_after = t > 0, t < spans - 1
    teams = spans // 4
    edge = jnp.logical_or(jnp.logical_and(seat == 0, has_before), jnp.logical_and(seat == 3, has_after))

    pieces = 4
    part = videos // pieces
    fetches = [
        pltpu.make_async_copy(a, b, sem_in.at[i])
        for i, (a, b) in enumerate(
            [(counts_hbm, cnt_s), (counts_hbm, cnt_v), (dest_hbm, dest_v)]
            + [(frames_hbm.at[pl.ds(q * part, part)], frames.at[pl.ds(q * part, part)]) for q in range(pieces)]
            + [(w1_hbm, w1), (w2_hbm, w2), (gain_hbm, gain), (bias_hbm, bias)]
        )
    ]
    for fetch in fetches:
        fetch.start()

    enc = (enc_0, enc_1)
    recv = (recv_0, recv_1)
    barrier = pltpu.get_barrier_semaphore()

    def greet(load, place):
        pl.semaphore_signal(barrier, inc=1, device_id=(load, place), device_id_type=MESH)

    @pl.when(edge)
    def _():
        greet(me, beyond)

    for s in range(1, 4):
        greet(me, team * 4 + lax.rem(seat + s, 4))

    for s in range(1, teams):

        @pl.when(team + s < teams)
        def _():
            greet(me, lax.rem(t + 4 * s, spans))

    @pl.loop(1, loads)
    def _(s):
        greet(lax.rem(me + s, loads), t)

    for fetch in fetches[:-3]:
        fetch.wait()

    @pl.loop(0, videos)
    def _(v):
        tail[0, v] = frames[v, jnp.clip(cnt_s[0, v] - 2, 0, length - 1)]
        tail[1, v] = frames[v, jnp.clip(cnt_s[0, v] - 1, 0, length - 1)]

    def products(g):
        at = pl.ds(g * group, group)
        lhs = jnp.concatenate([flat(tail[0, at]), flat(tail[1, at])], axis=1)
        t1_send[pl.ds(g * rows, rows)] = dot(lhs, w1[: 2 * channels]).astype(BF16)

    products(0)
    lanes = 128
    row = jnp.pad(dest_v[...], ((0, 7), (0, lanes - videos)), constant_values=-1)
    d_send[...] = row

    pl.semaphore_wait(barrier, 3 + (loads - 1) + jnp.where(edge, 1, 0) + team)

    for s in range(1, teams):

        @pl.when(team >= s)
        def _():
            pl.semaphore_signal(
                sem_ready.at[s - 1],
                inc=1,
                device_id=(me, lax.rem(t + spans - 4 * s, spans)),
                device_id_type=MESH,
            )

    def remote(src, dst, ss, rs, load, place):
        return pltpu.make_async_remote_copy(
            src_ref=src, dst_ref=dst, send_sem=ss, recv_sem=rs, device_id=(load, place), device_id_type=MESH
        )

    def context(g):
        place = pl.ds(pl.multiple_of(g * rows, rows), rows)
        return remote(t1_send.at[place], t1_recv.at[place], sem_c_send.at[g], sem_c_recv.at[g], me, after)

    for g in range(videos // group):
        if g > 0:
            products(g)

        @pl.when(has_after)
        def _():
            context(g).start()

    d_recv[me] = row

    def column(values):
        r = lax.broadcasted_iota(jnp.int32, (videos, videos), 0)
        c = lax.broadcasted_iota(jnp.int32, (videos, videos), 1)
        return jnp.sum(jnp.where(r == c, values, 0), axis=1, keepdims=True)

    for fetch in fetches[-3:]:
        fetch.wait()
    counts_row = cnt_v[...]

    def add_sums(g, at, values, fresh):
        tiles = values.reshape(group, places // 8, 8, channels)
        s1 = jnp.sum(tiles, axis=1)
        s2 = jnp.sum(tiles * tiles, axis=1)
        if fresh:
            acc1[at] = s1
            acc2[at] = s2
        else:
            acc1[at] += s1
            acc2[at] += s2

    def group_live(g, step, limit_of):
        parts = [limit_of(cnt_s[0, g * group + i]) > step for i in range(group)]
        return parts

    def masked(value, flags):
        pieces = value.reshape(group, places, channels)
        return jnp.concatenate(
            [jnp.where(flags[i], pieces[i : i + 1], 0.0) for i in range(group)], axis=0
        )

    @pl.loop(0, videos // group)
    def _(g):
        at = pl.ds(g * group, group)
        place = pl.ds(pl.multiple_of(g * rows, rows), rows)
        for j in range(1, 4):
            lhs = jnp.concatenate([flat(frames[at, 2 * j - 2 + k]) for k in range(3)], axis=1)
            value = masked(silu(dot(lhs, w1[...])), group_live(g, 2 * j, lambda n: n))
            value = value.reshape(rows, channels).astype(BF16)
            first[j, place] = value
            add_sums(g, at, value.astype(F32), j == 1)

    @pl.loop(1, loads)
    def _(s):
        remote(d_send, d_recv.at[me], sem_t.at[2], sem_t.at[3], lax.rem(me + s, loads), t).start()

    @pl.loop(0, videos // group)
    def _(g):
        at = pl.ds(g * group, group)
        place = pl.ds(pl.multiple_of(g * rows, rows), rows)

        @pl.when(has_before)
        def _():
            context(g).wait_recv()

        part = jnp.where(has_before, t1_recv[place].astype(F32), 0.0)
        value = silu(part + dot(flat(frames[at, 0]), w1[2 * channels :])).astype(BF16)
        first[0, place] = value
        add_sums(g, at, value.astype(F32), False)

    s1 = jnp.sum(acc1[...], axis=1)
    s2 = jnp.sum(acc2[...], axis=1)
    num = (((counts_row + 1) // 2) * places).astype(F32)
    num = jnp.pad(num, ((0, 7), (0, lanes - videos)))

    def parts(x):
        return [x[:, r * quarter : (r + 1) * quarter] for r in range(4)]

    for r, (p1, p2) in enumerate(zip(parts(s1), parts(s2))):
        a_send[r] = jnp.concatenate([jnp.concatenate([p1, p2], axis=1), num], axis=0)

    def mates(source, target, ss, rs):
        made = []
        for s in range(1, 4):
            mate = lax.rem(seat + s, 4)
            made.append(
                remote(source.at[mate], target.at[seat], ss.at[s - 1], rs.at[s - 1], me, team * 4 + mate)
            )
        return made

    a_copies = mates(a_send, a_recv, sem_a_send, sem_a_recv)
    for copy in a_copies:
        copy.start()
    a_recv[seat] = a_send[seat]

    place_of = column(dest_v[...])
    place_of = place_of // videos * 2 + place_of % 2
    lane = lax.broadcasted_iota(jnp.int32, (videos, 128), 1)
    video = lax.broadcasted_iota(jnp.int32, (videos, 128), 0)
    pack_v[...] = jnp.clip(jnp.sum(jnp.where(place_of == lane, video, 0), axis=0, keepdims=True), 0, videos - 1)
    to_scalars = pltpu.make_async_copy(pack_v, pack_s, sem_in.at[len(fetches)])
    to_scalars.start()

    my_gain = sum(jnp.where(seat == r, g, 0.0) for r, g in enumerate(parts(gain[...])))
    my_gain = jnp.concatenate([my_gain, my_gain], axis=1)
    for s in range(1, 4):
        from_mate = lax.rem(seat + 4 - s, 4)
        remote(
            a_send.at[0], a_recv.at[from_mate], sem_a_send.at[s - 1], sem_a_recv.at[s - 1], me, after
        ).wait_recv()
    totals = [a_recv[0]]
    for r in range(1, 4):
        totals.append(totals[-1] + a_recv[r])
    def totals_to(s):
        return remote(
            b_send, b_recv.at[s - 1], sem_b.at[0, s - 1], sem_b.at[1, s - 1], me, lax.rem(t + 4 * s, spans)
        )

    b_send[...] = totals[-1]
    for s in range(1, teams):

        @pl.when(team + s < teams)
        def _():
            pl.semaphore_wait(sem_ready.at[s - 1], 1)
            totals_to(s).start()

    base = jnp.zeros_like(totals[0])
    for s in range(teams - 1, 0, -1):

        @pl.when(team >= s)
        def _():
            totals_to(s).wait_recv()

        base = base + jnp.where(team >= s, b_recv[s - 1], 0.0)

    in_low = lax.broadcasted_iota(jnp.int32, (videos, lanes), 1) < quarter
    for r in range(4):
        total = base + totals[r]
        value = total[:videos] / column(total[videos : videos + 1, :videos])
        swapped = jnp.concatenate([value[:, quarter:], value[:, :quarter]], axis=1)
        var = value - swapped * swapped
        c_send[r] = jnp.where(in_low, value, lax.rsqrt(var + 1e-05) * my_gain)
    c_copies = mates(c_send, c_recv, sem_s_send, sem_s_recv)
    for copy in c_copies:
        copy.start()
    c_recv[seat] = c_send[seat]
    for s in range(1, 4):
        from_mate = lax.rem(seat + 4 - s, 4)
        remote(
            c_send.at[0], c_recv.at[from_mate], sem_s_send.at[s - 1], sem_s_recv.at[s - 1], me, after
        ).wait_recv()
    mean_v[...] = jnp.concatenate([c_recv[r][:, :quarter] for r in range(4)], axis=1)
    scale_v[...] = jnp.concatenate([c_recv[r][:, quarter:] for r in range(4)], axis=1)

    def exchange(i):
        stage[i, me, 0] = enc[i][pack_s[0, 2 * me]]
        stage[i, me, 1] = enc[i][pack_s[0, 2 * me + 1]]
        recv[i][me] = stage[i, me]

        @pl.loop(1, loads)
        def _(s):
            to = lax.rem(me + s, loads)
            stage[i, to, 0] = enc[i][pack_s[0, 2 * to]]
            stage[i, to, 1] = enc[i][pack_s[0, 2 * to + 1]]
            remote(stage.at[i, to], recv[i].at[me], sem_x_send.at[i], sem_x_recv.at[i], to, t).start()

    def all_of(i):
        sent = pl.ds(0, loads - 1)
        return remote(stage.at[i, sent], recv[i].at[sent], sem_x_send.at[i], sem_x_recv.at[i], me, after)

    @pl.loop(0, videos // group)
    def _(g):
        at = pl.ds(pl.multiple_of(g * group, group), group)
        place = pl.ds(pl.multiple_of(g * rows, rows), rows)
        mean = mean_v[at][:, None, :]
        scale = scale_v[at][:, None, :]
        taps = []
        for j in range(3):
            value = first[j, place].astype(F32).reshape(group, places, channels)
            value = ((value - mean) * scale).reshape(rows, channels).astype(BF16)
            first[j, place] = value
            taps.append(value)
        lhs = jnp.concatenate(taps, axis=1)
        value = masked(dot(lhs, w2[...]) + bias[...], group_live(g, 2, lambda n: (n + 1) // 2))
        enc_1[at] = value.astype(BF16)

    to_scalars.wait()
    exchange(1)

    @pl.loop(0, videos // group)
    def _(g):
        place = pl.ds(pl.multiple_of(g * rows, rows), rows)
        at = pl.ds(pl.multiple_of(g * group, group), group)
        normed = [first[j, place].astype(F32).reshape(group, places, channels) for j in range(4)]
        normed[3] = (normed[3] - mean_v[at][:, None, :]) * scale_v[at][:, None, :]
        ends = []
        for k in range(2):
            pieces = []
            for i in range(group):
                n = (cnt_s[0, g * group + i] + 1) // 2
                pieces.append(
                    jnp.where(
                        n == 2,
                        normed[k][i : i + 1],
                        jnp.where(n == 3, normed[k + 1][i : i + 1], normed[k + 2][i : i + 1]),
                    )
                )
            ends.append(jnp.concatenate(pieces, axis=0).reshape(rows, channels).astype(BF16))
        t2_send[place] = dot(jnp.concatenate(ends, axis=1), w2[: 2 * channels]).astype(BF16)

    t2 = remote(t2_send, t2_recv, sem_t.at[0], sem_t.at[1], me, after)

    @pl.when(has_after)
    def _():
        t2.start()


    @pl.when(has_before)
    def _():
        t2.wait_recv()

    @pl.loop(0, videos // group)
    def _(g):
        at = pl.ds(g * group, group)
        place = pl.ds(pl.multiple_of(g * rows, rows), rows)
        part = jnp.where(has_before, t2_recv[place].astype(F32), 0.0)
        value = part + dot(first[0, place], w2[2 * channels :]) + bias[...]
        enc_0[at] = value.reshape(group, places, channels).astype(BF16)

    exchange(0)

    others = pl.ds(0, loads - 1)
    remote(d_recv.at[others], d_recv.at[others], sem_t.at[2], sem_t.at[3], me, after).wait()
    known = d_recv[...][:, 0, :]
    loader = lax.broadcasted_iota(jnp.int32, known.shape, 0)
    for i in range(pairs):
        table[i] = jnp.clip(jnp.sum(jnp.where(known == me * videos + 2 * i, loader, 0)), 0, loads - 1)

    for copy in a_copies + c_copies:
        copy.wait_send()

    @pl.when(has_after)
    def _():
        for g in range(videos // group):
            context(g).wait_send()
        t2.wait_send()

    for s in range(1, teams):

        @pl.when(team + s < teams)
        def _():
            totals_to(s).wait_send()


    for i in (1, 0):
        all_of(i).wait_recv()

        @pl.loop(0, pairs)
        def _(q):
            out[2 * q, i] = recv[i][table[q], 0]
            out[2 * q + 1, i] = recv[i][table[q], 1]

        all_of(i).wait_send()


def body(loads, spans, frames, counts, dest, first_weight, second_weight, gain, bias):
    videos, length, places, channels = frames.shape[1:]
    group = min(16, videos)
    rows = videos * places
    vmem = pl.BlockSpec(memory_space=pltpu.VMEM)
    hbm = pl.BlockSpec(memory_space=pltpu.HBM)
    message = (videos + 8, 128)
    result = pl.pallas_call(
        functools.partial(kernel, loads, spans, group),
        out_shape=jax.ShapeDtypeStruct((videos, 2, places, channels), BF16),
        in_specs=[hbm] * 7,
        out_specs=vmem,
        scratch_shapes=[
            pltpu.SMEM((1, videos), jnp.int32),
            pltpu.VMEM((1, videos), jnp.int32),
            pltpu.VMEM((1, videos), jnp.int32),
            pltpu.VMEM((videos, length, places, channels), BF16),
            pltpu.VMEM((3 * channels, channels), BF16),
            pltpu.VMEM((3 * channels, channels), BF16),
            pltpu.VMEM((1, channels), F32),
            pltpu.VMEM((1, channels), F32),
            pltpu.VMEM((1, 128), jnp.int32),
            pltpu.SMEM((1, 128), jnp.int32),
            pltpu.VMEM((2, videos, places, channels), BF16),
            pltpu.VMEM((rows, channels), BF16),
            pltpu.VMEM((rows, channels), BF16),
            pltpu.VMEM((rows, channels), BF16),
            pltpu.VMEM((rows, channels), BF16),
            pltpu.VMEM((4, rows, channels), BF16),
            pltpu.VMEM((videos, 8, channels), F32),
            pltpu.VMEM((videos, 8, channels), F32),
            pltpu.VMEM((4,) + message, F32),
            pltpu.VMEM((4,) + message, F32),
            pltpu.VMEM(message, F32),
            pltpu.VMEM((spans // 4 - 1,) + message, F32),
            pltpu.VMEM((4, videos, 128), F32),
            pltpu.VMEM((4, videos, 128), F32),
            pltpu.VMEM((videos, channels), F32),
            pltpu.VMEM((videos, channels), F32),
            pltpu.VMEM((videos, places, channels), BF16),
            pltpu.VMEM((videos, places, channels), BF16),
            pltpu.VMEM((2, loads, 2, places, channels), BF16),
            pltpu.VMEM((loads, 2, places, channels), BF16),
            pltpu.VMEM((loads, 2, places, channels), BF16),
            pltpu.VMEM((8, 128), jnp.int32),
            pltpu.VMEM((loads, 8, 128), jnp.int32),
            pltpu.SMEM((videos // 2,), jnp.int32),
            pltpu.SemaphoreType.DMA((12,)),
            pltpu.SemaphoreType.DMA((4,)),
            pltpu.SemaphoreType.DMA((videos // group,)),
            pltpu.SemaphoreType.DMA((videos // group,)),
            pltpu.SemaphoreType.DMA((3,)),
            pltpu.SemaphoreType.DMA((3,)),
            pltpu.SemaphoreType.REGULAR((spans // 4 - 1,)),
            pltpu.SemaphoreType.DMA((2, spans // 4 - 1)),
            pltpu.SemaphoreType.DMA((3,)),
            pltpu.SemaphoreType.DMA((3,)),
            pltpu.SemaphoreType.DMA((2,)),
            pltpu.SemaphoreType.DMA((2,)),
        ],
        compiler_params=pltpu.CompilerParams(
            collective_id=0, has_side_effects=True, vmem_limit_bytes=48 * 1024 * 1024
        ),
    )(
        *(
            pltpu.with_memory_space_constraint(operand, pltpu.HBM)
            for operand in (
                counts,
                dest.reshape(1, videos),
                frames[0],
                first_weight.reshape(3 * channels, channels),
                second_weight.reshape(3 * channels, channels),
                gain.reshape(1, channels),
                bias.reshape(1, channels),
            )
        )
    )
    return result[None]


def solution(mesh):
    loads, spans = mesh.shape["load"], mesh.shape["tm"]
    return jax.shard_map(
        functools.partial(body, loads, spans),
        mesh=mesh,
        in_specs=(
            P("tm", "load", None, None, None),
            P("tm", "load"),
            P("load"),
            P(),
            P(),
            P(),
            P(),
        ),
        out_specs=P("tm", "load", None, None, None),
        check_vma=False,
    )
```
